128 devices in a mesh: attn: 2 (over core), expert: 64 (over z, x, y).
Axes of the slice: x: 4, y: 4, z: 4, core: 2. Of those that a mesh axis runs over, the one named last changes fastest.
Arguments:
- queries: bfloat16 [1024, 36864], P(('attn', 'expert')), may hold values from -200 to 200, as said below
- new_latent: bfloat16 [1024, 576], P(('attn', 'expert')), may hold values from -6 to 6
- latent_cache: bfloat16 [2048, 36864], P(('attn', 'expert')), may hold values from -6 to 6
- block_table: int32 [128, 16], P(('attn', 'expert')), may hold values from 0 to 15, each once within a row
- lengths: int32 [128, 8], P(('attn', 'expert')), may hold values from 1 to 128, 576 in all within a row
- value_up: bfloat16 [64, 512, 128], P('expert'), may hold values from -0.25 to 0.25
- out_proj: bfloat16 [8192, 3584], P('expert'), may hold values from -0.0625 to 0.0625
- norm_gain: float32 [3584], replicated, may hold values from 0.1 to 1.9
- expert_ids: int32 [1024, 8], P(('attn', 'expert')), may hold values from 0 to 127, all different within a row; in each aligned block of 8 rows (0 to 7, 8 to 15, ...) at most 2 rows name the same one
- affinity: float32 [1024, 8], P(('attn', 'expert')), may hold values from 0.02 to 1
- gate_weight: bfloat16 [128, 3584, 1024], P('expert', None, 'attn'), may hold values from -0.09375 to 0.09375
- up_weight: bfloat16 [128, 3584, 1024], P('expert', None, 'attn'), may hold values from -0.09375 to 0.09375
- down_weight: bfloat16 [128, 1024, 3584], P('expert', 'attn'), may hold values from -0.1875 to 0.1875
Outputs:
- normed: bfloat16 [1024, 3584], P(('attn', 'expert'))
- expert_out: bfloat16 [1024, 3584], P(('attn', 'expert'))
The draws below stay inside these ranges and needn't reach their ends.
Inputs may be any that keep to these rules, and one draw needn't show every extreme that they name: Absorbed queries; some heads of some tokens may carry large scales. `block_table`: each row lists every page of its device's pool once; sequence s of the device owns entries s * 2 to (s + 1) * 2 - 1, in position order. `lengths`: on each device the longest sequence holds exactly 128 cached entries. `expert_ids`: A token names 8 different experts; among the 8 tokens of one device no expert is named by more than 2 tokens, a bound that some block reaches.
All inputs are finite; a program needn't handle non-finite values.
Results may differ from the reference program's by a relative error of at most 0.022.
Values may be sent and summed in bfloat16 or wider, within the bound.
No kernel may reach another device: no remote copies, remote signals or barrier semaphores. Data moves between devices by JAX's collectives and lax.ppermute only.
A program may use at most 128 MiB of HBM per device.

```python
import math
import jax
import jax.numpy as jnp
import numpy as np
from jax import lax

D = 3584
FF = 1024
KV = 512
ROPE = 64
VHEAD = 128
TOP = 8
PAGE = 64
SEQ_DEV = 8
PAGES_SEQ = 2
ENTRY = 576
EXPERTS = 128
HEADS = 64
TOKENS = 1024
POOL = 16
CAP = 2
N_ATTN = 2
N_EXPERT = 64


def draw_queries(key, part):
    key = jax.random.fold_in(key, 11)
    base = jnp.clip(jax.random.normal(key, (TOKENS, HEADS, KV + ROPE), jnp.float32), -4.0, 4.0)
    return base.reshape(TOKENS, HEADS * (KV + ROPE)).astype(jnp.bfloat16)


def steps_of(key, dims, pieces, low, top_value):
    def one(axis_at, shards_of):
        draws = jax.random.uniform(jax.random.fold_in(jax.random.fold_in(key, 6), axis_at), (shards_of,), jnp.float32, low / len(pieces), top_value / len(pieces))
        return jnp.repeat(jnp.exp(draws), dims[axis_at] // shards_of).reshape((-1,) + (1,) * (len(dims) - axis_at - 1))

    factor_of = one(*pieces[0])
    for cut in pieces[1:]:
        factor_of = factor_of * one(*cut)
    return factor_of


def profile(count, total, reach, slope):
    weights = [(1 << 20) // math.isqrt(grade ** slope) + 1 for grade in range(2, count + 1)]
    surplus, given = total - reach - (count - 1), [1] * (count - 1)
    while surplus > 0:
        movable = [i for i in range(count - 1) if given[i] < reach]
        pool, budget = sum([weights[i] for i in movable]), surplus
        for i in movable:
            addition = min(reach - given[i], max(1, budget * weights[i] // pool), surplus)
            given[i] = given[i] + addition
            surplus = surplus - addition
    return np.array([reach] + given)


def ragged(stream_key, count, total, reach, lean):
    if count == 2:
        one = jax.random.randint(stream_key, (), max(1, total - reach), min(reach, total - 1) + 1)
        return jnp.stack([one, total - one])
    sizes = jnp.asarray(profile(count, total, reach, lean), jnp.int32)
    twos = (count - 1) // 2
    giver, sink = sizes[1:1 + 2 * twos:2], sizes[2:2 + 2 * twos:2]
    room = jnp.minimum(giver - 1, reach - sink)
    shifted = jax.random.randint(jax.random.fold_in(stream_key, 1), (twos,), 0, 1 << 20) % (room + 1)
    sizes = sizes.at[1:1 + 2 * twos:2].set(giver - shifted).at[2:2 + 2 * twos:2].set(sink + shifted)
    return sizes[jax.random.permutation(jax.random.fold_in(stream_key, 2), count)]


def shared_out(own_key, own, number, rows, amount, top, most, skew):
    ranking = jax.random.permutation(own_key, amount)
    heavy_load, common = shares(amount, rows * top, most, skew, True), shares(amount, rows * top, most, skew, False)
    places = jnp.arange(amount)

    def named(tallies, turn):
        used = int((tallies > 0).sum())
        fixed = max(1, used // 4)
        passed = fixed + (places - fixed + turn * (used - fixed)) % max(1, amount - fixed)
        return jnp.zeros((amount,), jnp.int32).at[ranking[jnp.where(places < fixed, places, passed)]].set(jnp.asarray(tallies, jnp.int32))

    tallies = jnp.where(number % 4 == 0, named(heavy_load, number // 4), named(common, number - number // 4 - 1))
    mixed = jax.random.permutation(jax.random.fold_in(own, 3), amount)
    source_of, taker = mixed[0:amount // 2 * 2:2], mixed[1:amount // 2 * 2:2]
    margin = jnp.minimum(tallies[source_of] - 1, most - tallies[taker]) // 2
    margin = jnp.where((source_of == ranking[0]) | (taker == ranking[0]) | (tallies[taker] == 0), 0, jnp.maximum(margin, 0))
    passed = jax.random.randint(jax.random.fold_in(own, 4), (amount // 2,), 0, 1 << 20) % (margin + 1)
    tallies = tallies.at[source_of].add(-passed).at[taker].add(passed)
    members = jnp.searchsorted(jnp.cumsum(tallies), jnp.arange(rows * top), side="right").astype(jnp.int32)
    grid = members.reshape(top, rows).T
    grid = grid[jax.random.permutation(jax.random.fold_in(own, 1), rows)]
    turn = jax.random.randint(jax.random.fold_in(own, 2), (rows, 1), 0, top)
    return jnp.take_along_axis(grid, (jnp.arange(top)[None, :] + turn) % top, axis=1)


def shares(count, total, bound, skew, full):
    loads = [(1 << 20) // math.isqrt(standing ** skew) + 1 for standing in range(1, count + 1)]
    largest = bound if full else min(bound, max(-(-total // count), total * loads[0] // sum(loads)))
    least = 1 if total - largest >= count - 1 else 0
    counts, rest = [largest] + [least] * (count - 1), total - largest - least * (count - 1)
    while rest > 0:
        movable = [i for i in range(1, count) if counts[i] < largest] or [i for i in range(1, count) if counts[i] < bound]
        mass, left = sum([loads[i] for i in movable]), rest
        for i in movable:
            extra = min(bound - counts[i], max(1, left * loads[i] // mass), rest)
            counts[i] = counts[i] + extra
            rest = rest - extra
    return np.array(counts)


def gaussian(key, dims, spread, reach, cuts=(), kind=jnp.bfloat16):
    result = jax.random.normal(key, dims, jnp.float32) * spread
    if len(cuts) > 0:
        result = steps_of(key, dims, cuts, -0.22, 0.18) * result
    return jnp.clip(result, min=-reach, max=reach).astype(kind)


def setup_inputs(seed: int = 0) -> dict:
    splits = jax.random.split(jax.random.key(seed), 14)
    queries = draw_queries(jax.random.fold_in(splits[13], 71), 0)
    new_latent = gaussian(splits[1], (TOKENS, ENTRY), 1.0, 6.0, ((0, 128),))
    latent_cache = gaussian(splits[2], (N_ATTN * N_EXPERT * POOL, PAGE * ENTRY), 1.0, 6.0, ((0, 128),))
    block_table = jax.vmap(lambda own: jax.random.permutation(own, POOL))(jax.random.split(splits[3], (N_ATTN * N_EXPERT))).reshape((N_ATTN * N_EXPERT, POOL)).astype(jnp.int32)
    lengths = jax.vmap(lambda own: ragged(own, SEQ_DEV, (SEQ_DEV + 1) * PAGES_SEQ * PAGE // 2, PAGES_SEQ * PAGE, 2))(jax.random.split(splits[4], (N_ATTN * N_EXPERT))).reshape((N_ATTN * N_EXPERT, SEQ_DEV)).astype(jnp.int32)
    value_up = gaussian(splits[5], (HEADS, KV, VHEAD), KV ** -0.5, 0.25, ((0, 64),))
    out_proj = gaussian(splits[6], (HEADS * VHEAD, D), (HEADS * VHEAD) ** -0.5, 0.0625, ((0, 64),))
    norm_gain = jnp.clip(1.0 + 0.18 * jax.random.normal(splits[7], (D,), jnp.float32), 0.1, 1.9)
    expert_ids_keys = jax.random.split(jax.random.fold_in(splits[8], 1), TOKENS // SEQ_DEV)
    expert_ids_turns = jax.random.permutation(jax.random.fold_in(splits[8], 3), TOKENS // SEQ_DEV)
    expert_ids = jax.vmap(lambda own, number: shared_out(jax.random.fold_in(splits[8], 2), own, number, SEQ_DEV, EXPERTS, TOP, CAP, 2))(expert_ids_keys, expert_ids_turns).reshape((TOKENS, TOP))
    affinity = jnp.clip(jnp.exp(math.log(1.0) - 3.912023 * jax.random.uniform(splits[9], (TOKENS, TOP), jnp.float32) ** steps_of(splits[9], (TOKENS, TOP), ((0, 128),), -0.2, 0.2)), 0.02, 1.0)
    gate_weight = gaussian(splits[10], (EXPERTS, D, FF), D ** -0.5, 0.09375, ((0, 64), (2, 2)))
    up_weight = gaussian(splits[11], (EXPERTS, D, FF), D ** -0.5, 0.09375, ((0, 64), (2, 2)))
    down_weight = gaussian(splits[12], (EXPERTS, FF, D), FF ** -0.5, 0.1875, ((0, 64), (1, 2)))
    return dict(queries=queries, new_latent=new_latent, latent_cache=latent_cache, block_table=block_table, lengths=lengths, value_up=value_up, out_proj=out_proj, norm_gain=norm_gain, expert_ids=expert_ids, affinity=affinity, gate_weight=gate_weight, up_weight=up_weight, down_weight=down_weight)


SCORE_SCALE = 192.0 ** (-0.5)
ROUTED_SCALE = 2.5
EPSILON = 1e-06

def attend_rows(query_rows, fresh_latent, key_rows, live_count, kv_width):
    scores = jnp.einsum('she,sje->shj', query_rows, key_rows) * SCORE_SCALE
    own_score = jnp.einsum('she,se->sh', query_rows, fresh_latent) * SCORE_SCALE
    positions = jnp.arange(key_rows.shape[1], dtype=jnp.int32)
    live_mask = positions[None, None, :] < live_count[:, None, None]
    scores = jnp.where(live_mask, scores, -jnp.inf)
    highest = jnp.maximum(lax.optimization_barrier(jnp.max(scores, axis=2)), own_score)
    raised = jnp.exp(scores - highest[:, :, None])
    own_raised = jnp.exp(own_score - highest)
    denominator = lax.optimization_barrier(jnp.sum(raised, axis=2)) + own_raised
    weights = (raised / denominator[:, :, None]).astype(jnp.bfloat16).astype(jnp.float32)
    own_weight = (own_raised / denominator).astype(jnp.bfloat16).astype(jnp.float32)
    latent = jnp.einsum('shj,sjc->shc', weights, key_rows[:, :, :kv_width])
    latent = latent + own_weight[:, :, None] * fresh_latent[:, None, :kv_width]
    return latent.astype(jnp.bfloat16)

def reference(queries, new_latent, latent_cache, block_table, lengths, value_up, out_proj, norm_gain, expert_ids, affinity, gate_weight, up_weight, down_weight):
    device_count = N_ATTN * N_EXPERT
    entry_width = KV + ROPE
    pool_pages = SEQ_DEV * PAGES_SEQ
    context = PAGES_SEQ * PAGE

    def one_device(device_index):
        first_row = device_index * SEQ_DEV
        query_rows = lax.dynamic_slice_in_dim(queries, first_row, SEQ_DEV, 0)
        query_rows = query_rows.reshape(SEQ_DEV, HEADS, entry_width).astype(jnp.float32)
        fresh_latent = lax.dynamic_slice_in_dim(new_latent, first_row, SEQ_DEV, 0).astype(jnp.float32)
        page_table = lax.dynamic_index_in_dim(block_table, device_index, 0, keepdims=False) + device_index * pool_pages
        key_rows = jnp.take(latent_cache, page_table.astype(jnp.int32), axis=0)
        key_rows = key_rows.reshape(SEQ_DEV, context, entry_width).astype(jnp.float32)
        live_count = lax.dynamic_index_in_dim(lengths, device_index, 0, keepdims=False)
        return attend_rows(query_rows, fresh_latent, key_rows, live_count, KV)
    latent = lax.map(one_device, jnp.arange(device_count, dtype=jnp.int32))
    latent = latent.reshape(TOKENS, HEADS, KV).astype(jnp.float32)
    values = jnp.einsum('thc,hcv->thv', latent, value_up.astype(jnp.float32)).astype(jnp.bfloat16)
    values = values.reshape(TOKENS, HEADS * VHEAD)
    attn_out = jnp.dot(values, out_proj, preferred_element_type=jnp.float32)
    mean_square = lax.optimization_barrier(jnp.mean(attn_out * attn_out, axis=1, keepdims=True))
    normed = (attn_out * lax.rsqrt(mean_square + EPSILON) * norm_gain).astype(jnp.bfloat16)
    pair_ids = expert_ids.reshape(device_count, SEQ_DEV * TOP)
    onehot = (pair_ids[:, :, None] == jnp.arange(EXPERTS, dtype=jnp.int32)[None, None, :]).astype(jnp.int32)
    slot_rank = lax.optimization_barrier(jnp.sum((jnp.cumsum(onehot, axis=1) - 1) * onehot, axis=2)).astype(jnp.int32)
    flat_expert = pair_ids.reshape(-1).astype(jnp.int32)
    flat_rank = slot_rank.reshape(-1)
    token_index = jnp.arange(TOKENS * TOP, dtype=jnp.int32) // TOP
    device_of = token_index // SEQ_DEV
    buffer = jnp.zeros((EXPERTS, device_count, CAP, D), jnp.bfloat16)
    buffer = buffer.at[flat_expert, device_of, flat_rank].set(normed[token_index])

    def run_expert(operands):
        expert_rows, gate_part, up_part, down_part = operands
        expert_in = expert_rows.reshape(device_count * CAP, D).astype(jnp.float32)
        gate_proj = jnp.dot(expert_in, gate_part.astype(jnp.float32))
        up_proj = jnp.dot(expert_in, up_part.astype(jnp.float32))
        hidden = (jax.nn.silu(gate_proj) * up_proj).astype(jnp.bfloat16)
        reply = jnp.dot(hidden.astype(jnp.float32), down_part.astype(jnp.float32)).astype(jnp.bfloat16)
        return reply.reshape(device_count, CAP, D)
    replies = lax.map(run_expert, (buffer, gate_weight, up_weight, down_weight))
    picked = replies[flat_expert, device_of, flat_rank].reshape(TOKENS, TOP, D)
    route_weight = affinity / lax.optimization_barrier(jnp.sum(affinity, axis=1, keepdims=True)) * ROUTED_SCALE
    expert_out = lax.optimization_barrier(jnp.sum(route_weight[:, :, None] * picked.astype(jnp.float32), axis=1)).astype(jnp.bfloat16)
    return (normed, expert_out)
```

```python
import jax
import jax.numpy as jnp
from jax import lax
from jax.sharding import Mesh, PartitionSpec as P

SCORE_SCALE = 192.0 ** (-0.5)
ROUTED_SCALE = 2.5
EPSILON = 1e-06
SIDE = 4
CHIPS = ("z", "x", "y")
SWAP = [(0, 1), (1, 0)]


def attend_rows(query_rows, fresh_latent, key_rows, live_count, kv_width):
    scores = (
        jnp.einsum("she,sje->shj", query_rows, key_rows, preferred_element_type=jnp.float32)
        * SCORE_SCALE
    )
    own_score = (
        jnp.einsum("she,se->sh", query_rows, fresh_latent, preferred_element_type=jnp.float32)
        * SCORE_SCALE
    )
    positions = jnp.arange(key_rows.shape[1], dtype=jnp.int32)
    live_mask = positions[None, None, :] < live_count[:, None, None]
    scores = jnp.where(live_mask, scores, -jnp.inf)
    highest = jnp.maximum(jnp.max(scores, axis=2), own_score)
    raised = jnp.exp(scores - highest[:, :, None])
    own_raised = jnp.exp(own_score - highest)
    denominator = jnp.sum(raised, axis=2) + own_raised
    weights = (raised / denominator[:, :, None]).astype(jnp.bfloat16)
    own_weight = (own_raised / denominator).astype(jnp.bfloat16)
    latent = jnp.einsum(
        "shj,sjc->shc", weights, key_rows[:, :, :kv_width], preferred_element_type=jnp.float32
    )
    latent = latent + own_weight.astype(jnp.float32)[:, :, None] * fresh_latent[
        :, None, :kv_width
    ].astype(jnp.float32)
    return latent.astype(jnp.bfloat16)


def along_y(array, step):
    return lax.ppermute(array, "y", [(i, (i + step) % SIDE) for i in range(SIDE)])


def other_core(array):
    return lax.ppermute(array, "core", SWAP)


def expert_rows(arrived_rows, gate_weight, up_weight, down_weight):
    gate_proj = jnp.einsum(
        "secd,edf->secf", arrived_rows, gate_weight, preferred_element_type=jnp.float32
    )
    up_proj = jnp.einsum(
        "secd,edf->secf", arrived_rows, up_weight, preferred_element_type=jnp.float32
    )
    hidden = (jax.nn.silu(gate_proj) * up_proj).astype(jnp.bfloat16)
    return jnp.einsum("secf,efd->secd", hidden, down_weight, preferred_element_type=jnp.float32)


def shards(
    queries,
    new_latent,
    latent_cache,
    block_table,
    lengths,
    value_up,
    out_proj,
    norm_gain,
    expert_ids,
    affinity,
    gate_weight,
    up_weight,
    down_weight,
):
    seq_count, entry_width = new_latent.shape
    head_count = queries.shape[1] // entry_width
    kv_width = value_up.shape[1]
    pool_pages = latent_cache.shape[0]
    context = pool_pages // seq_count * (latent_cache.shape[1] // entry_width)
    model_width = out_proj.shape[1]
    half = model_width // 2
    core = lax.axis_index("core")
    place_y = lax.axis_index("y")
    planes = head_count // SIDE

    part = lax.dynamic_slice_in_dim(out_proj, core * half, half, 1)
    mine = [along_y(part, k) for k in range(1, SIDE)]
    theirs = [other_core(m) for m in mine]
    ups = [value_up[0]] + [along_y(value_up[0], k) for k in range(1, SIDE)]

    key_rows = jnp.take(latent_cache, block_table.reshape(-1), axis=0).reshape(
        seq_count, context, entry_width
    )
    query_rows = queries.reshape(seq_count, head_count, entry_width)
    latent = attend_rows(query_rows, new_latent, key_rows, lengths.reshape(-1), kv_width)
    outbound = jnp.transpose(latent, (1, 0, 2)).reshape(planes, SIDE * seq_count, kv_width)
    arrived = lax.all_to_all(outbound, ("z", "x"), split_axis=0, concat_axis=0, tiled=True)
    arrived = arrived.reshape(planes, SIDE, seq_count, kv_width)
    total = jnp.zeros((planes * seq_count, model_width), jnp.float32)
    for k in range(SIDE):
        rows = lax.dynamic_index_in_dim(
            arrived, lax.rem(place_y - k + SIDE, SIDE), 1, keepdims=False
        ).reshape(planes * seq_count, kv_width)
        values = jnp.dot(rows, ups[k], preferred_element_type=jnp.float32).astype(jnp.bfloat16)
        if k == 0:
            weight = out_proj
        else:
            first = jnp.where(core == 0, mine[k - 1], theirs[k - 1])
            second = jnp.where(core == 0, theirs[k - 1], mine[k - 1])
            weight = jnp.concatenate([first, second], axis=1)
        total = total + jnp.dot(values, weight, preferred_element_type=jnp.float32)
    partial = total.astype(jnp.bfloat16).reshape(planes, seq_count, model_width)
    collected = lax.all_to_all(partial, ("z", "x"), split_axis=0, concat_axis=0, tiled=True)
    attn_out = jnp.sum(collected.astype(jnp.float32), axis=0)
    mean_square = jnp.mean(attn_out * attn_out, axis=1, keepdims=True)
    normed = (attn_out * lax.rsqrt(mean_square + EPSILON) * norm_gain).astype(jnp.bfloat16)

    chip_count = SIDE**3
    local_experts = gate_weight.shape[0]
    expert_count = chip_count * local_experts
    top_count = expert_ids.shape[1]
    capacity = max(2, 2 * seq_count * top_count // expert_count)
    pair_ids = expert_ids.reshape(-1)
    onehot = (pair_ids[:, None] == jnp.arange(expert_count, dtype=jnp.int32)[None, :]).astype(
        jnp.int32
    )
    slot_rank = jnp.sum((jnp.cumsum(onehot, axis=0) - 1) * onehot, axis=1)
    slot_index = pair_ids * capacity + slot_rank
    slot_table = slot_index.reshape(seq_count, top_count)
    slot_numbers = jnp.arange(expert_count * capacity, dtype=jnp.int32)
    placement = jnp.any(slot_table[None, :, :] == slot_numbers[:, None, None], axis=2).astype(
        jnp.bfloat16
    )
    outgoing = jnp.dot(placement, normed, preferred_element_type=jnp.float32).astype(jnp.bfloat16)
    outgoing = outgoing.reshape(chip_count, local_experts * capacity, model_width)
    received = lax.all_to_all(outgoing, CHIPS, split_axis=0, concat_axis=0, tiled=True)
    both = jnp.concatenate([received, other_core(received)], axis=0)
    both = both.reshape(2 * chip_count, local_experts, capacity, model_width)
    partial_value = expert_rows(both, gate_weight, up_weight, down_weight)
    partial_value = partial_value.reshape(2, chip_count, local_experts * capacity, model_width)
    beside = other_core(partial_value[1].astype(jnp.bfloat16))
    reply = (partial_value[0] + beside.astype(jnp.float32)).astype(jnp.bfloat16)
    returned = lax.all_to_all(reply, CHIPS, split_axis=0, concat_axis=0, tiled=True)
    returned_rows = returned.reshape(expert_count * capacity, model_width)
    picked = jnp.take(returned_rows, slot_index, axis=0).reshape(seq_count, top_count, model_width)
    route_weight = affinity / jnp.sum(affinity, axis=1, keepdims=True) * ROUTED_SCALE
    expert_out = jnp.sum(route_weight[:, :, None] * picked.astype(jnp.float32), axis=1).astype(
        jnp.bfloat16
    )
    return (normed, expert_out)


def solution(mesh):
    grid = Mesh(mesh.devices.reshape(2, SIDE, SIDE, SIDE), ("core",) + CHIPS)
    rows = P(("core",) + CHIPS, None)
    placed = (
        rows,
        rows,
        rows,
        rows,
        rows,
        P(CHIPS, None, None),
        P(CHIPS, None),
        P(),
        rows,
        rows,
        P(CHIPS, None, "core"),
        P(CHIPS, None, "core"),
        P(CHIPS, "core", None),
    )
    return jax.shard_map(
        shards, mesh=grid, in_specs=placed, out_specs=(rows, rows), check_vma=False
    )
```

```python
import jax
import jax.numpy as jnp
from jax import lax
from jax.experimental import pallas as pl
from jax.experimental.pallas import tpu as pltpu
from jax.sharding import Mesh, PartitionSpec as P

SCORE_SCALE = 192.0 ** (-0.5)
ROUTED_SCALE = 2.5
EPSILON = 1e-06
SIDE = 4
CHIPS = ("z", "x", "y")
SWAP = [(0, 1), (1, 0)]
F32 = jnp.float32
BF16 = jnp.bfloat16
MIB = 1 << 20
SMEM = pl.BlockSpec(memory_space=pltpu.SMEM)
VMEM = pl.BlockSpec(memory_space=pltpu.VMEM)
HBM = pl.BlockSpec(memory_space=pltpu.HBM)


def dot_nt(a, b):
    return lax.dot_general(a, b, (((1,), (1,)), ((), ())), preferred_element_type=F32)


def dot(a, b):
    return jnp.dot(a, b, preferred_element_type=F32)


def attend_kernel(
    table_hbm, length_hbm, query_hbm, fresh_hbm, cache_hbm, out_ref,
    table_ref, length_ref, query_ref, fresh_ref, cache_ref, key_ref, sems,
):
    moves = (
        (cache_hbm, cache_ref),
        (query_hbm, query_ref),
        (table_hbm, table_ref),
        (length_hbm, length_ref),
        (fresh_hbm, fresh_ref),
    )
    copies = [pltpu.make_async_copy(a, b, sems.at[i]) for i, (a, b) in enumerate(moves)]
    for copy in copies:
        copy.start()
    seq_count, entry = fresh_ref.shape
    pages = cache_ref.shape[0]
    pairs = cache_ref.shape[1] // (2 * entry)
    wide = entry + 64
    kv_width = out_ref.shape[1]
    spots = pairs * pages
    copies[0].wait()
    for r in range(pairs):
        at = 2 * entry * r
        key_ref[0, r * pages : (r + 1) * pages, :] = cache_ref[:, at : at + wide]
        key_ref[1, r * pages : (r + 1) * pages, :] = cache_ref[:, at + entry - 64 : at + 2 * entry]
    even_keys, odd_keys = key_ref[0], key_ref[1]

    for copy in copies[1:]:
        copy.wait()
    sequence = lax.broadcasted_iota(jnp.int32, (seq_count, spots), 0)
    lane = lax.broadcasted_iota(jnp.int32, (seq_count, spots), 1)
    page, entry_at = lane % pages, 2 * (lane // pages)
    first = jnp.zeros((seq_count, spots), jnp.int32)
    second, live = first, first
    for s in range(seq_count):
        here = sequence == s
        first = jnp.where(here, table_ref[0, 2 * s], first)
        second = jnp.where(here, table_ref[0, 2 * s + 1], second)
        live = jnp.where(here, length_ref[0, s], live)

    def bias_of(position):
        inside = ((page == first) & (position < live)) | (
            (page == second) & (position + 2 * pairs < live)
        )
        return jnp.where(inside, 0.0, -jnp.inf).astype(F32)

    even_bias, odd_bias = bias_of(entry_at), bias_of(entry_at + 1)
    fresh = jnp.concatenate(
        [fresh_ref[...].astype(F32), jnp.zeros((seq_count, wide - entry), F32)], axis=1
    )
    group = 8
    for g in range(query_ref.shape[1] // (2 * entry) // group):
        base = 2 * entry * group * g
        evens = [
            query_ref[:, base + 2 * entry * i : base + 2 * entry * i + wide].astype(F32)
            for i in range(group)
        ]
        odds = [
            query_ref[:, base + 2 * entry * (i + 1) - wide : base + 2 * entry * (i + 1)].astype(F32)
            for i in range(group)
        ]
        rows = group * seq_count
        column = lax.broadcasted_iota(jnp.int32, (rows, wide), 1)
        even_low = jnp.where(column < entry, jnp.concatenate(evens, axis=0), 0.0)
        odd_high = jnp.where(column >= 64, jnp.concatenate(odds, axis=0), 0.0)
        even_high = pltpu.roll(even_low, 64, 1)
        odd_low = pltpu.roll(odd_high, entry, 1)
        low = jnp.concatenate([even_low, odd_low], axis=0)
        high = jnp.concatenate([even_high, odd_high], axis=0)
        heads = 2 * group
        own = jnp.sum(
            low.reshape(heads, seq_count, wide) * fresh[None], axis=2, keepdims=True
        ) * SCORE_SCALE
        even_scores = (dot_nt(low.astype(BF16), even_keys) * SCORE_SCALE).reshape(
            heads, seq_count, spots
        ) + even_bias[None]
        odd_scores = (dot_nt(high.astype(BF16), odd_keys) * SCORE_SCALE).reshape(
            heads, seq_count, spots
        ) + odd_bias[None]
        top = jnp.maximum(
            jnp.max(jnp.maximum(even_scores, odd_scores), axis=2, keepdims=True), own
        )
        even_raised = jnp.exp(even_scores - top)
        odd_raised = jnp.exp(odd_scores - top)
        own_raised = jnp.exp(own - top)
        scale = 1.0 / (
            jnp.sum(even_raised + odd_raised, axis=2, keepdims=True) + own_raised
        )
        even_weights = (even_raised * scale).astype(BF16).reshape(2 * rows, spots)
        odd_weights = (odd_raised * scale).astype(BF16).reshape(2 * rows, spots)
        own_weight = (own_raised * scale).astype(BF16).astype(F32)
        even_part = dot(even_weights, even_keys)[:, :kv_width]
        odd_part = pltpu.roll(dot(odd_weights, odd_keys), entry, 1)[:, :kv_width]
        own_part = (own_weight * fresh[None, :, :kv_width]).reshape(2 * rows, kv_width)
        latent = even_part + odd_part + own_part
        for i in range(group):
            two = jnp.concatenate(
                [
                    latent[i * seq_count : (i + 1) * seq_count],
                    latent[rows + i * seq_count : rows + (i + 1) * seq_count],
                ],
                axis=0,
            )
            at = 2 * seq_count * (group * g + i)
            out_ref[at : at + 2 * seq_count, :] = two.astype(BF16)


def attend(block_table, lengths, queries, new_latent, latent_cache, kv_width):
    seq_count, entry = new_latent.shape
    head_count = queries.shape[1] // entry
    pages, page_width = latent_cache.shape
    spots = pages * page_width // (2 * entry)
    return pl.pallas_call(
        attend_kernel,
        out_shape=jax.ShapeDtypeStruct((head_count * seq_count, kv_width), BF16),
        in_specs=[HBM] * 5,
        out_specs=VMEM,
        scratch_shapes=[
            pltpu.SMEM(block_table.shape, jnp.int32),
            pltpu.SMEM(lengths.shape, jnp.int32),
            pltpu.VMEM(queries.shape, BF16),
            pltpu.VMEM(new_latent.shape, BF16),
            pltpu.VMEM(latent_cache.shape, BF16),
            pltpu.VMEM((2, spots, entry + 64), BF16),
            pltpu.SemaphoreType.DMA((5,)),
        ],
        compiler_params=pltpu.CompilerParams(vmem_limit_bytes=60 * MIB),
        cost_estimate=pl.CostEstimate(
            flops=1_400_000_000, bytes_accessed=2_400_000, transcendentals=600_000
        ),
        name="attend",
    )(block_table, lengths, queries, new_latent, latent_cache)


def prepare_kernel(
    out_proj, value_up, ids_hbm, affinity_hbm, top, bottom, routes, ids, affinity, sems
):
    core = lax.axis_index("core")
    head_rows, half = out_proj.shape[0], out_proj.shape[1] // 2
    at = pl.ds(pl.multiple_of(core * half, 128), half)
    middle = head_rows // 2
    moves = [(ids_hbm, ids), (affinity_hbm, affinity)]
    for i, part in enumerate((top, bottom)):
        moves.append((out_proj.at[pl.ds(i * middle, middle), at], part.at[:, :half]))
        for b in range(value_up.shape[1] // head_rows):
            rows = pl.ds(b * head_rows + i * middle, middle)
            columns = pl.ds(half + b * head_rows, head_rows)
            moves.append((value_up.at[0, rows], part.at[:, columns]))
    copies = [pltpu.make_async_copy(a, b, sems.at[i]) for i, (a, b) in enumerate(moves)]
    for copy in copies:
        copy.start()
    for copy in copies[:2]:
        copy.wait()
    rows, top_count = ids.shape
    rest = jnp.zeros((rows, routes.shape[1] - 2 * top_count), F32)
    routes[...] = jnp.concatenate([ids[...].astype(F32), affinity[...], rest], axis=1)
    for copy in copies[2:]:
        copy.wait()


def prepare(out_proj, value_up, expert_ids, affinity):
    head_rows, width = out_proj.shape
    return pl.pallas_call(
        prepare_kernel,
        out_shape=(
            jax.ShapeDtypeStruct((head_rows // 2, width // 2 + value_up.shape[1]), BF16),
            jax.ShapeDtypeStruct((head_rows // 2, width // 2 + value_up.shape[1]), BF16),
            jax.ShapeDtypeStruct((expert_ids.shape[0], 128), F32),
        ),
        in_specs=[HBM] * 4,
        out_specs=(VMEM, VMEM, VMEM),
        scratch_shapes=[
            pltpu.VMEM(expert_ids.shape, jnp.int32),
            pltpu.VMEM(affinity.shape, F32),
            pltpu.SemaphoreType.DMA((4 + 2 * (value_up.shape[1] // head_rows),)),
        ],
        compiler_params=pltpu.CompilerParams(vmem_limit_bytes=60 * MIB),
        cost_estimate=pl.CostEstimate(flops=0, bytes_accessed=1_200_000, transcendentals=0),
        name="prepare",
    )(out_proj, value_up, expert_ids, affinity)


def route_kernel(own_ref, far_ref, place_ref, mix_ref):
    core = lax.axis_index("core")
    seq_count = own_ref.shape[0]
    tokens, top_count = 2 * seq_count, 8
    columns = place_ref.shape[1]
    routes = jnp.concatenate([own_ref[...], far_ref[...]], axis=0)
    affinity = routes[:, top_count : 2 * top_count]
    share = affinity / jnp.sum(affinity, axis=1, keepdims=True) * ROUTED_SCALE
    experts = routes.shape[1]
    expert = lax.broadcasted_iota(jnp.int32, (tokens, experts), 1).astype(F32)
    chosen = jnp.zeros((tokens, experts), F32)
    shares = jnp.zeros((tokens, experts), F32)
    for k in range(top_count):
        hit = expert == routes[:, k : k + 1]
        chosen = jnp.where(hit, 1.0, chosen)
        shares = jnp.where(hit, share[:, k : k + 1], shares)
    row = lax.broadcasted_iota(jnp.int32, (tokens, tokens), 0)
    column = lax.broadcasted_iota(jnp.int32, (tokens, tokens), 1)
    earlier = ((column < row) & (column // seq_count == row // seq_count)).astype(F32)
    rank = dot(earlier.astype(BF16), chosen.astype(BF16))
    token = lax.broadcasted_iota(jnp.int32, (tokens, experts), 0)
    slot = (rank + jnp.where(token < seq_count, 1.0, 3.0)) * chosen
    named = lax.broadcasted_iota(jnp.int32, (experts, columns), 0)
    at = lax.broadcasted_iota(jnp.int32, (experts, columns), 1)
    spread = (named == at // 8 * 2 + core).astype(F32).astype(BF16)
    high = shares.astype(BF16)
    low = (shares - high.astype(F32)).astype(BF16)
    at = lax.broadcasted_iota(jnp.int32, (tokens, columns), 1)
    filled = dot(slot.astype(BF16), spread) == (at % 4 + 1).astype(F32)
    high = jnp.where(filled, dot(high, spread), 0.0)
    low = jnp.where(filled, dot(low, spread), 0.0)
    placed = filled.astype(F32)
    first = at % 8 < 4

    def by_half(table):
        return [jnp.where(first, table, 0.0), jnp.where(first, 0.0, table)]

    place_ref[...] = jnp.concatenate(by_half(placed), axis=0).astype(BF16)
    mix_ref[...] = jnp.concatenate(by_half(high) + by_half(low), axis=0).astype(BF16)


def route(own, far, chips):
    tokens = 2 * own.shape[0]
    return pl.pallas_call(
        route_kernel,
        out_shape=(
            jax.ShapeDtypeStruct((2 * tokens, chips * 8), BF16),
            jax.ShapeDtypeStruct((4 * tokens, chips * 8), BF16),
        ),
        in_specs=[VMEM] * 2,
        out_specs=(VMEM, VMEM),
        compiler_params=pltpu.CompilerParams(vmem_limit_bytes=8 * MIB),
        cost_estimate=pl.CostEstimate(
            flops=20_000_000, bytes_accessed=120_000, transcendentals=0
        ),
        name="route",
    )(own, far)


def value_kernel(arrived_ref, *refs):
    *piece_refs, out_ref = refs
    place_y = lax.axis_index("y")
    rows, kv_width = arrived_ref.shape
    tokens = rows // SIDE
    head_rows = 2 * piece_refs[0].shape[0]
    half = piece_refs[0].shape[1] - kv_width
    to = lax.broadcasted_iota(jnp.int32, (tokens, rows), 0)
    source = lax.broadcasted_iota(jnp.int32, (tokens, rows), 1)
    plane, seq = to // 8, to % 8
    arrived = arrived_ref[...]
    ups = [
        jnp.concatenate([piece_refs[2 * k][:, half:], piece_refs[2 * k + 1][:, half:]], axis=0)
        for k in range(SIDE)
    ]
    for k, up in enumerate(ups):
        head = lax.rem(place_y - k + SIDE, SIDE)
        pick = (source == plane * (SIDE * 8) + head * 8 + seq).astype(F32)
        latent = dot(pick.astype(BF16), arrived).astype(BF16)
        total = jnp.zeros((tokens, head_rows), F32)
        for at in range(0, kv_width, head_rows):
            total = total + dot(latent[:, at : at + head_rows], up[:, at : at + head_rows])
        out_ref[:, k * head_rows : (k + 1) * head_rows] = total.astype(BF16)


def find_values(arrived, pieces):
    rows = arrived.shape[0]
    return pl.pallas_call(
        value_kernel,
        out_shape=jax.ShapeDtypeStruct((rows // SIDE, 2 * SIDE * pieces[0].shape[0]), BF16),
        in_specs=[VMEM] * 9,
        out_specs=VMEM,
        compiler_params=pltpu.CompilerParams(vmem_limit_bytes=12 * MIB),
        cost_estimate=pl.CostEstimate(
            flops=350_000_000, bytes_accessed=3_200_000, transcendentals=0
        ),
        name="find_values",
    )(arrived, *pieces)


def project_kernel(own_values, far_values, *refs):
    *piece_refs, out_ref = refs
    rows, width = own_values.shape
    head_rows = 2 * piece_refs[0].shape[0]
    half = out_ref.shape[1]
    to = lax.broadcasted_iota(jnp.int32, (2 * rows, rows), 0)
    source = lax.broadcasted_iota(jnp.int32, (2 * rows, rows), 1)
    same = source == to // 16 * 8 + to % 8
    near = (same & (to % 16 < 8)).astype(F32).astype(BF16)
    far = (same & (to % 16 >= 8)).astype(F32).astype(BF16)
    values = (dot(near, own_values[...]) + dot(far, far_values[...])).astype(BF16)
    step = 256
    for at in range(0, half, step):
        total = jnp.zeros((2 * rows, step), F32)
        columns = slice(at, at + step)
        for k in range(SIDE):
            part = jnp.concatenate(
                [piece_refs[2 * k][:, columns], piece_refs[2 * k + 1][:, columns]], axis=0
            )
            total = total + dot(values[:, k * head_rows : (k + 1) * head_rows], part)
        out_ref[:, at : at + step] = total.astype(BF16)


def project(own_values, far_values, pieces, half):
    return pl.pallas_call(
        project_kernel,
        out_shape=jax.ShapeDtypeStruct((2 * own_values.shape[0], half), BF16),
        in_specs=[VMEM] * 10,
        out_specs=VMEM,
        compiler_params=pltpu.CompilerParams(vmem_limit_bytes=12 * MIB),
        cost_estimate=pl.CostEstimate(
            flops=600_000_000, bytes_accessed=3_000_000, transcendentals=0
        ),
        name="project",
    )(own_values, far_values, *pieces)


def expert_kernel(
    rows_ref, gate_ref, up_ref, down_ref, gate_far, up_far, down_far, out_ref,
    gate_buf, up_buf, down_buf, wide_ref, total_ref, sems,
):
    core = lax.axis_index("core")
    blocks, width, block = gate_buf.shape
    half = width // 2
    count = total_ref.shape[0]

    def copies(i):
        near = i < blocks // 2
        at = pl.ds((i % (blocks // 2)) * block, block)
        gate, up, down = (gate_ref, up_ref, down_ref) if near else (gate_far, up_far, down_far)
        return (
            pltpu.make_async_copy(gate.at[core, :, at], gate_buf.at[i], sems.at[0, i]),
            pltpu.make_async_copy(up.at[core, :, at], up_buf.at[i], sems.at[1, i]),
            pltpu.make_async_copy(down.at[core, at, :], down_buf.at[i], sems.at[2, i]),
        )

    started = [copies(i) for i in range(blocks)]
    for three in started:
        for copy in three:
            copy.start()

    to = lax.broadcasted_iota(jnp.int32, (count, 2 * count), 0)
    source = lax.broadcasted_iota(jnp.int32, (count, 2 * count), 1)
    step = 256
    for side in range(2):
        pick = (source == to // 4 * 8 + to % 4 + 4 * side).astype(F32).astype(BF16)
        for at in range(0, half, step):
            wide_ref[:, side * half + at : side * half + at + step] = dot(
                pick, rows_ref[:, at : at + step]
            ).astype(BF16)

    for i in range(blocks):
        started[i][0].wait()
        started[i][1].wait()
        gate = dot(wide_ref[...], gate_buf[i])
        up = dot(wide_ref[...], up_buf[i])
        hidden = (gate / (1.0 + jnp.exp(-gate)) * up).astype(BF16)
        started[i][2].wait()
        for at in range(0, width, 2 * step):
            part = dot(hidden, down_buf[i, :, at : at + 2 * step])
            if i == 0:
                total_ref[:, at : at + 2 * step] = part
            else:
                total_ref[:, at : at + 2 * step] += part

    to = lax.broadcasted_iota(jnp.int32, (2 * count, count), 0)
    source = lax.broadcasted_iota(jnp.int32, (2 * count, count), 1)
    first = (to % 8 < 4) & (source == to // 8 * 4 + to % 4)
    second = (to % 8 >= 4) & (source == to // 8 * 4 + to % 4)
    first = first.astype(F32).astype(BF16)
    second = second.astype(F32).astype(BF16)
    for at in range(0, half, step):
        out_ref[:, at : at + step] = (
            dot(first, total_ref[:, at : at + step].astype(BF16))
            + dot(second, total_ref[:, half + at : half + at + step].astype(BF16))
        ).astype(BF16)


def run_expert(rows, near, far):
    width = near[2].shape[2]
    hidden = near[2].shape[1]
    block = 256
    blocks = 2 * hidden // block
    count = rows.shape[0] // 2
    return pl.pallas_call(
        expert_kernel,
        out_shape=jax.ShapeDtypeStruct(rows.shape, BF16),
        in_specs=[VMEM] + [HBM] * 6,
        out_specs=VMEM,
        scratch_shapes=[
            pltpu.VMEM((blocks, width, block), BF16),
            pltpu.VMEM((blocks, width, block), BF16),
            pltpu.VMEM((blocks, block, width), BF16),
            pltpu.VMEM((count, width), BF16),
            pltpu.VMEM((count, width), F32),
            pltpu.SemaphoreType.DMA((3, blocks)),
        ],
        compiler_params=pltpu.CompilerParams(vmem_limit_bytes=57 * MIB),
        cost_estimate=pl.CostEstimate(
            flops=7_500_000_000, bytes_accessed=26_000_000, transcendentals=300_000
        ),
        name="expert",
    )(rows, *near, *far)


def along_y(array, step):
    return lax.ppermute(array, "y", [(i, (i + step) % SIDE) for i in range(SIDE)])


def other_core(array):
    return lax.ppermute(array, "core", SWAP)


def shards(
    queries,
    new_latent,
    latent_cache,
    block_table,
    lengths,
    value_up,
    out_proj,
    norm_gain,
    expert_ids,
    affinity,
    gate_weight,
    up_weight,
    down_weight,
):
    seq_count = new_latent.shape[0]
    kv_width = value_up.shape[1]
    head_rows, model_width = out_proj.shape
    half = model_width // 2
    core = lax.axis_index("core")
    planes = SIDE * SIDE
    chips = SIDE**3

    top, bottom, routes = prepare(out_proj, value_up, expert_ids, affinity)
    one_top, three_bottom = along_y(top, 1), along_y(bottom, -1)
    far_routes = other_core(routes)

    latent = attend(block_table, lengths, queries, new_latent, latent_cache, kv_width)
    outbound = latent.reshape(planes, SIDE * seq_count, kv_width)
    outbound, one_top, three_bottom, far_routes = lax.optimization_barrier(
        (outbound, one_top, three_bottom, far_routes)
    )
    two_top, two_bottom = along_y(one_top, 1), along_y(three_bottom, -1)
    one_bottom, three_top = along_y(bottom, 1), along_y(top, -1)
    pieces = (top, bottom, one_top, one_bottom, two_top, two_bottom, three_top, three_bottom)
    arrived = lax.all_to_all(outbound, ("z", "x"), split_axis=0, concat_axis=0, tiled=True)
    arrived = arrived.reshape(planes * SIDE * seq_count, kv_width)
    placement, mixing = route(routes, far_routes, chips)
    arrived, placement, mixing = lax.optimization_barrier((arrived, placement, mixing))

    own_values = find_values(arrived, pieces)
    partial = project(own_values, other_core(own_values), pieces, half)
    partial, gate_weight = lax.optimization_barrier((partial, gate_weight))
    far_gate = other_core(gate_weight)
    partial = partial.reshape(planes, 2 * seq_count, half)
    collected = lax.all_to_all(partial, ("z", "x"), split_axis=0, concat_axis=0, tiled=True)
    mine = jnp.sum(collected.astype(F32), axis=0)
    theirs = other_core(mine)
    theirs = jnp.concatenate([theirs[seq_count:], theirs[:seq_count]], axis=0)
    attn_out = jnp.where(
        core == 0,
        jnp.concatenate([mine, theirs], axis=1),
        jnp.concatenate([theirs, mine], axis=1),
    )
    attn_out, up_weight, down_weight = lax.optimization_barrier(
        (attn_out, up_weight, down_weight)
    )
    far_weights = (far_gate, other_core(up_weight), other_core(down_weight))
    weights = (gate_weight, up_weight, down_weight)
    mean_square = jnp.mean(attn_out * attn_out, axis=1, keepdims=True)
    both = (attn_out * lax.rsqrt(mean_square + EPSILON) * norm_gain).astype(BF16)
    normed = both[:seq_count]
    both = jnp.concatenate([both[:, :half], both[:, half:]], axis=0)
    outgoing = lax.dot_general(
        placement, both, (((0,), (0,)), ((), ())), preferred_element_type=F32
    )
    outgoing = outgoing.astype(BF16).reshape(chips, 8, half)
    received = lax.all_to_all(outgoing, CHIPS, split_axis=0, concat_axis=0, tiled=True)
    reply = run_expert(received.reshape(chips * 8, half), weights, far_weights)
    returned = lax.all_to_all(
        reply.reshape(chips, 8, half), CHIPS, split_axis=0, concat_axis=0, tiled=True
    )
    mixed = dot(mixing, returned.reshape(chips * 8, half))
    mixed = mixed[: 4 * seq_count] + mixed[4 * seq_count :]
    mixed = mixed.reshape(2, 2, seq_count, half)
    mixed = jnp.transpose(mixed, (1, 2, 0, 3)).reshape(2, seq_count, model_width)
    expert_out = (mixed[0] + other_core(mixed[1])).astype(BF16)
    return (normed, expert_out)


def solution(mesh):
    grid = Mesh(mesh.devices.reshape(2, SIDE, SIDE, SIDE), ("core",) + CHIPS)
    rows = P(("core",) + CHIPS, None)
    placed = (
        rows,
        rows,
        rows,
        rows,
        rows,
        P(CHIPS, None, None),
        P(CHIPS, None),
        P(),
        rows,
        rows,
        P(CHIPS, None, "core"),
        P(CHIPS, None, "core"),
        P(CHIPS, "core", None),
    )
    return jax.shard_map(
        shards, mesh=grid, in_specs=placed, out_specs=(rows, rows), check_vma=False
    )
```

```python
import jax
import jax.numpy as jnp
from jax import lax
from jax.experimental import pallas as pl
from jax.experimental.pallas import tpu as pltpu
from jax.sharding import Mesh, PartitionSpec as P

SCORE_SCALE = 192.0 ** (-0.5)
ROUTED_SCALE = 2.5
EPSILON = 1e-06
SIDE = 4
CHIPS = ("z", "x", "y")
SWAP = [(0, 1), (1, 0)]
F32 = jnp.float32
BF16 = jnp.bfloat16
MIB = 1 << 20
SMEM = pl.BlockSpec(memory_space=pltpu.SMEM)
VMEM = pl.BlockSpec(memory_space=pltpu.VMEM)
HBM = pl.BlockSpec(memory_space=pltpu.HBM)


def dot_nt(a, b):
    return lax.dot_general(a, b, (((1,), (1,)), ((), ())), preferred_element_type=F32)


def dot(a, b):
    return jnp.dot(a, b, preferred_element_type=F32)


def attend_kernel(
    table_hbm, length_hbm, query_hbm, fresh_hbm, cache_hbm, out_ref,
    table_ref, length_ref, query_ref, fresh_ref, cache_ref, key_ref, sems,
):
    moves = (
        (cache_hbm, cache_ref),
        (query_hbm, query_ref),
        (table_hbm, table_ref),
        (length_hbm, length_ref),
        (fresh_hbm, fresh_ref),
    )
    copies = [pltpu.make_async_copy(a, b, sems.at[i]) for i, (a, b) in enumerate(moves)]
    for copy in copies:
        copy.start()
    seq_count, entry = fresh_ref.shape
    pages = cache_ref.shape[0]
    pairs = cache_ref.shape[1] // (2 * entry)
    wide = entry + 64
    kv_width = out_ref.shape[1]
    spots = pairs * pages
    copies[0].wait()
    for r in range(pairs):
        at = 2 * entry * r
        key_ref[0, r * pages : (r + 1) * pages, :] = cache_ref[:, at : at + wide]
        key_ref[1, r * pages : (r + 1) * pages, :] = cache_ref[:, at + entry - 64 : at + 2 * entry]
    even_keys, odd_keys = key_ref[0], key_ref[1]

    for copy in copies[1:]:
        copy.wait()
    sequence = lax.broadcasted_iota(jnp.int32, (seq_count, spots), 0)
    lane = lax.broadcasted_iota(jnp.int32, (seq_count, spots), 1)
    page, entry_at = lane % pages, 2 * (lane // pages)
    first = jnp.zeros((seq_count, spots), jnp.int32)
    second, live = first, first
    for s in range(seq_count):
        here = sequence == s
        first = jnp.where(here, table_ref[0, 2 * s], first)
        second = jnp.where(here, table_ref[0, 2 * s + 1], second)
        live = jnp.where(here, length_ref[0, s], live)

    def bias_of(position):
        inside = ((page == first) & (position < live)) | (
            (page == second) & (position + 2 * pairs < live)
        )
        return jnp.where(inside, 0.0, -jnp.inf).astype(F32)

    even_bias, odd_bias = bias_of(entry_at), bias_of(entry_at + 1)
    fresh = jnp.concatenate(
        [fresh_ref[...].astype(F32), jnp.zeros((seq_count, wide - entry), F32)], axis=1
    )
    group = 8
    for g in range(query_ref.shape[1] // (2 * entry) // group):
        base = 2 * entry * group * g
        evens = [
            query_ref[:, base + 2 * entry * i : base + 2 * entry * i + wide].astype(F32)
            for i in range(group)
        ]
        odds = [
            query_ref[:, base + 2 * entry * (i + 1) - wide : base + 2 * entry * (i + 1)].astype(F32)
            for i in range(group)
        ]
        rows = group * seq_count
        column = lax.broadcasted_iota(jnp.int32, (rows, wide), 1)
        even_low = jnp.where(column < entry, jnp.concatenate(evens, axis=0), 0.0)
        odd_high = jnp.where(column >= 64, jnp.concatenate(odds, axis=0), 0.0)
        even_high = pltpu.roll(even_low, 64, 1)
        odd_low = pltpu.roll(odd_high, entry, 1)
        low = jnp.concatenate([even_low, odd_low], axis=0)
        high = jnp.concatenate([even_high, odd_high], axis=0)
        heads = 2 * group
        own = jnp.sum(
            low.reshape(heads, seq_count, wide) * fresh[None], axis=2, keepdims=True
        ) * SCORE_SCALE
        even_scores = (dot_nt(low.astype(BF16), even_keys) * SCORE_SCALE).reshape(
            heads, seq_count, spots
        ) + even_bias[None]
        odd_scores = (dot_nt(high.astype(BF16), odd_keys) * SCORE_SCALE).reshape(
            heads, seq_count, spots
        ) + odd_bias[None]
        top = jnp.maximum(
            jnp.max(jnp.maximum(even_scores, odd_scores), axis=2, keepdims=True), own
        )
        even_raised = jnp.exp(even_scores - top)
        odd_raised = jnp.exp(odd_scores - top)
        own_raised = jnp.exp(own - top)
        scale = 1.0 / (
            jnp.sum(even_raised + odd_raised, axis=2, keepdims=True) + own_raised
        )
        even_weights = (even_raised * scale).astype(BF16).reshape(2 * rows, spots)
        odd_weights = (odd_raised * scale).astype(BF16).reshape(2 * rows, spots)
        own_weight = (own_raised * scale).astype(BF16).astype(F32)
        even_part = dot(even_weights, even_keys)[:, :kv_width]
        odd_part = pltpu.roll(dot(odd_weights, odd_keys), entry, 1)[:, :kv_width]
        own_part = (own_weight * fresh[None, :, :kv_width]).reshape(2 * rows, kv_width)
        latent = even_part + odd_part + own_part
        for i in range(group):
            two = jnp.concatenate(
                [
                    latent[i * seq_count : (i + 1) * seq_count],
                    latent[rows + i * seq_count : rows + (i + 1) * seq_count],
                ],
                axis=0,
            )
            at = 2 * seq_count * (group * g + i)
            out_ref[at : at + 2 * seq_count, :] = two.astype(BF16)


def attend(block_table, lengths, queries, new_latent, latent_cache, kv_width):
    seq_count, entry = new_latent.shape
    head_count = queries.shape[1] // entry
    pages, page_width = latent_cache.shape
    spots = pages * page_width // (2 * entry)
    return pl.pallas_call(
        attend_kernel,
        out_shape=jax.ShapeDtypeStruct((head_count * seq_count, kv_width), BF16),
        in_specs=[HBM] * 5,
        out_specs=VMEM,
        scratch_shapes=[
            pltpu.SMEM(block_table.shape, jnp.int32),
            pltpu.SMEM(lengths.shape, jnp.int32),
            pltpu.VMEM(queries.shape, BF16),
            pltpu.VMEM(new_latent.shape, BF16),
            pltpu.VMEM(latent_cache.shape, BF16),
            pltpu.VMEM((2, spots, entry + 64), BF16),
            pltpu.SemaphoreType.DMA((5,)),
        ],
        compiler_params=pltpu.CompilerParams(vmem_limit_bytes=60 * MIB),
        cost_estimate=pl.CostEstimate(
            flops=1_400_000_000, bytes_accessed=2_400_000, transcendentals=600_000
        ),
        name="attend",
    )(block_table, lengths, queries, new_latent, latent_cache)


def prepare_kernel(out_proj, value_up, ids_hbm, affinity_hbm, piece, routes, ids, affinity, sems):
    core = lax.axis_index("core")
    head_rows, half = out_proj.shape[0], out_proj.shape[1] // 2
    at = pl.ds(pl.multiple_of(core * half, 128), half)
    moves = [
        (ids_hbm, ids),
        (affinity_hbm, affinity),
        (out_proj.at[:, at], piece.at[:, :half]),
    ]
    for b in range(value_up.shape[1] // head_rows):
        rows = pl.ds(b * head_rows, head_rows)
        columns = pl.ds(half + b * head_rows, head_rows)
        moves.append((value_up.at[0, rows], piece.at[:, columns]))
    copies = [pltpu.make_async_copy(a, b, sems.at[i]) for i, (a, b) in enumerate(moves)]
    for copy in copies:
        copy.start()
    for copy in copies[:2]:
        copy.wait()
    rows, top_count = ids.shape
    rest = jnp.zeros((rows, routes.shape[1] - 2 * top_count), F32)
    routes[...] = jnp.concatenate([ids[...].astype(F32), affinity[...], rest], axis=1)
    for copy in copies[2:]:
        copy.wait()


def prepare(out_proj, value_up, expert_ids, affinity):
    head_rows, width = out_proj.shape
    return pl.pallas_call(
        prepare_kernel,
        out_shape=(
            jax.ShapeDtypeStruct((head_rows, width // 2 + value_up.shape[1]), BF16),
            jax.ShapeDtypeStruct((expert_ids.shape[0], 128), F32),
        ),
        in_specs=[HBM] * 4,
        out_specs=(VMEM, VMEM),
        scratch_shapes=[
            pltpu.VMEM(expert_ids.shape, jnp.int32),
            pltpu.VMEM(affinity.shape, F32),
            pltpu.SemaphoreType.DMA((3 + value_up.shape[1] // head_rows,)),
        ],
        compiler_params=pltpu.CompilerParams(vmem_limit_bytes=60 * MIB),
        cost_estimate=pl.CostEstimate(flops=0, bytes_accessed=1_200_000, transcendentals=0),
        name="prepare",
    )(out_proj, value_up, expert_ids, affinity)


def route_kernel(own_ref, far_ref, place_ref, mix_ref):
    core = lax.axis_index("core")
    seq_count = own_ref.shape[0]
    tokens, top_count = 2 * seq_count, 8
    columns = place_ref.shape[1]
    routes = jnp.concatenate([own_ref[...], far_ref[...]], axis=0)
    affinity = routes[:, top_count : 2 * top_count]
    share = affinity / jnp.sum(affinity, axis=1, keepdims=True) * ROUTED_SCALE
    experts = routes.shape[1]
    expert = lax.broadcasted_iota(jnp.int32, (tokens, experts), 1).astype(F32)
    chosen = jnp.zeros((tokens, experts), F32)
    shares = jnp.zeros((tokens, experts), F32)
    for k in range(top_count):
        hit = expert == routes[:, k : k + 1]
        chosen = jnp.where(hit, 1.0, chosen)
        shares = jnp.where(hit, share[:, k : k + 1], shares)
    row = lax.broadcasted_iota(jnp.int32, (tokens, tokens), 0)
    column = lax.broadcasted_iota(jnp.int32, (tokens, tokens), 1)
    earlier = ((column < row) & (column // seq_count == row // seq_count)).astype(F32)
    rank = dot(earlier.astype(BF16), chosen.astype(BF16))
    token = lax.broadcasted_iota(jnp.int32, (tokens, experts), 0)
    slot = (rank + jnp.where(token < seq_count, 1.0, 3.0)) * chosen
    named = lax.broadcasted_iota(jnp.int32, (experts, columns), 0)
    at = lax.broadcasted_iota(jnp.int32, (experts, columns), 1)
    spread = (named == at // 8 * 2 + core).astype(F32).astype(BF16)
    high = shares.astype(BF16)
    low = (shares - high.astype(F32)).astype(BF16)
    at = lax.broadcasted_iota(jnp.int32, (tokens, columns), 1)
    filled = dot(slot.astype(BF16), spread) == (at % 4 + 1).astype(F32)
    high = jnp.where(filled, dot(high, spread), 0.0)
    low = jnp.where(filled, dot(low, spread), 0.0)
    placed = filled.astype(F32)
    first = at % 8 < 4

    def by_half(table):
        return [jnp.where(first, table, 0.0), jnp.where(first, 0.0, table)]

    place_ref[...] = jnp.concatenate(by_half(placed), axis=0).astype(BF16)
    mix_ref[...] = jnp.concatenate(by_half(high) + by_half(low), axis=0).astype(BF16)


def route(own, far, chips):
    tokens = 2 * own.shape[0]
    return pl.pallas_call(
        route_kernel,
        out_shape=(
            jax.ShapeDtypeStruct((2 * tokens, chips * 8), BF16),
            jax.ShapeDtypeStruct((4 * tokens, chips * 8), BF16),
        ),
        in_specs=[VMEM] * 2,
        out_specs=(VMEM, VMEM),
        compiler_params=pltpu.CompilerParams(vmem_limit_bytes=8 * MIB),
        cost_estimate=pl.CostEstimate(
            flops=20_000_000, bytes_accessed=120_000, transcendentals=0
        ),
        name="route",
    )(own, far)


def value_kernel(arrived_ref, *refs):
    *piece_refs, out_ref = refs
    place_y = lax.axis_index("y")
    rows, kv_width = arrived_ref.shape
    tokens = rows // SIDE
    head_rows = piece_refs[0].shape[0]
    half = piece_refs[0].shape[1] - kv_width
    to = lax.broadcasted_iota(jnp.int32, (tokens, rows), 0)
    source = lax.broadcasted_iota(jnp.int32, (tokens, rows), 1)
    plane, seq = to // 8, to % 8
    arrived = arrived_ref[...]
    own, one, top, bottom, three = piece_refs
    for k in range(SIDE):
        head = lax.rem(place_y - k + SIDE, SIDE)
        pick = (source == plane * (SIDE * 8) + head * 8 + seq).astype(F32)
        latent = dot(pick.astype(BF16), arrived).astype(BF16)
        total = jnp.zeros((tokens, head_rows), F32)
        for at in range(0, kv_width, head_rows):
            columns = slice(half + at, half + at + head_rows)
            if k == 2:
                up = jnp.concatenate([top[:, columns], bottom[:, columns]], axis=0)
            else:
                up = (own, one, None, three)[k][:, columns]
            total = total + dot(latent[:, at : at + head_rows], up)
        out_ref[:, k * head_rows : (k + 1) * head_rows] = total.astype(BF16)


def find_values(arrived, pieces):
    rows = arrived.shape[0]
    return pl.pallas_call(
        value_kernel,
        out_shape=jax.ShapeDtypeStruct((rows // SIDE, SIDE * pieces[0].shape[0]), BF16),
        in_specs=[VMEM] * 6,
        out_specs=VMEM,
        compiler_params=pltpu.CompilerParams(vmem_limit_bytes=12 * MIB),
        cost_estimate=pl.CostEstimate(
            flops=350_000_000, bytes_accessed=3_200_000, transcendentals=0
        ),
        name="find_values",
    )(arrived, *pieces)


def project_kernel(own_values, far_values, *refs):
    own, one, top, bottom, three, out_ref = refs
    rows = own_values.shape[0]
    head_rows = own.shape[0]
    half = out_ref.shape[1]
    to = lax.broadcasted_iota(jnp.int32, (2 * rows, rows), 0)
    source = lax.broadcasted_iota(jnp.int32, (2 * rows, rows), 1)
    same = source == to // 16 * 8 + to % 8
    near = (same & (to % 16 < 8)).astype(F32).astype(BF16)
    far = (same & (to % 16 >= 8)).astype(F32).astype(BF16)
    values = (dot(near, own_values[...]) + dot(far, far_values[...])).astype(BF16)
    step = 256
    for at in range(0, half, step):
        total = jnp.zeros((2 * rows, step), F32)
        columns = slice(at, at + step)
        two = jnp.concatenate([top[:, columns], bottom[:, columns]], axis=0)
        for k, part in enumerate((own[:, columns], one[:, columns], two, three[:, columns])):
            total = total + dot(values[:, k * head_rows : (k + 1) * head_rows], part)
        out_ref[:, at : at + step] = total.astype(BF16)


def project(own_values, far_values, pieces, half):
    return pl.pallas_call(
        project_kernel,
        out_shape=jax.ShapeDtypeStruct((2 * own_values.shape[0], half), BF16),
        in_specs=[VMEM] * 7,
        out_specs=VMEM,
        compiler_params=pltpu.CompilerParams(vmem_limit_bytes=12 * MIB),
        cost_estimate=pl.CostEstimate(
            flops=600_000_000, bytes_accessed=3_000_000, transcendentals=0
        ),
        name="project",
    )(own_values, far_values, *pieces)


def expert_kernel(
    rows_hbm, gate_far, up_far, down_far, gate_near, up_near, down_near, out_hbm,
    rows_ref, out_ref, gate_buf, up_buf, down_buf, wide_ref, total_ref, sems, edge_sems,
):
    core = lax.axis_index("core")
    blocks, width, block = gate_buf.shape
    half = width // 2
    count = total_ref.shape[0]

    def copies(i):
        near = i < blocks // 2
        gate, up, down = (gate_near, up_near, down_near) if near else (gate_far, up_far, down_far)
        at = pl.ds((i % (blocks // 2)) * block, block)
        return (
            pltpu.make_async_copy(gate.at[core, :, at], gate_buf.at[i], sems.at[0, i]),
            pltpu.make_async_copy(up.at[core, :, at], up_buf.at[i], sems.at[1, i]),
            pltpu.make_async_copy(down.at[core, at, :], down_buf.at[i], sems.at[2, i]),
        )

    step = 256
    edges = range(0, half, step)

    def chunk(at):
        return slice(None), pl.ds(at, step)

    arriving = [
        pltpu.make_async_copy(rows_hbm.at[chunk(at)], rows_ref.at[chunk(at)], edge_sems.at[0, i])
        for i, at in enumerate(edges)
    ]
    leaving = [
        pltpu.make_async_copy(out_ref.at[chunk(at)], out_hbm.at[chunk(at)], edge_sems.at[1, i])
        for i, at in enumerate(edges)
    ]
    for copy in arriving:
        copy.start()
    started = [copies(i) for i in range(blocks)]
    started[0][0].start()
    started[0][1].start()

    to = lax.broadcasted_iota(jnp.int32, (count, 2 * count), 0)
    source = lax.broadcasted_iota(jnp.int32, (count, 2 * count), 1)
    picks = [
        (source == to // 4 * 8 + to % 4 + 4 * side).astype(F32).astype(BF16) for side in range(2)
    ]
    for i, at in enumerate(edges):
        arriving[i].wait()
        for side in range(2):
            wide_ref[:, side * half + at : side * half + at + step] = dot(
                picks[side], rows_ref[:, at : at + step]
            ).astype(BF16)

    started[0][2].start()
    for copy in started[1]:
        copy.start()

    for i in range(blocks):
        started[i][0].wait()
        started[i][1].wait()
        if i + 2 < blocks:
            for copy in started[i + 2]:
                copy.start()
        gate = dot(wide_ref[...], gate_buf[i])
        up = dot(wide_ref[...], up_buf[i])
        hidden = (gate / (1.0 + jnp.exp(-gate)) * up).astype(BF16)
        started[i][2].wait()
        for at in range(0, width, 2 * step):
            part = dot(hidden, down_buf[i, :, at : at + 2 * step])
            if i == 0:
                total_ref[:, at : at + 2 * step] = part
            else:
                total_ref[:, at : at + 2 * step] += part

    to = lax.broadcasted_iota(jnp.int32, (2 * count, count), 0)
    source = lax.broadcasted_iota(jnp.int32, (2 * count, count), 1)
    same = source == to // 8 * 4 + to % 4
    first = ((to % 8 < 4) & same).astype(F32).astype(BF16)
    second = ((to % 8 >= 4) & same).astype(F32).astype(BF16)
    for i, at in enumerate(edges):
        out_ref[:, at : at + step] = (
            dot(first, total_ref[:, at : at + step].astype(BF16))
            + dot(second, total_ref[:, half + at : half + at + step].astype(BF16))
        ).astype(BF16)
        leaving[i].start()
    for copy in leaving:
        copy.wait()


def run_expert(rows, near, far):
    _, hidden, width = near[2].shape
    count, block = rows.shape[0] // 2, 256
    blocks = 2 * hidden // block
    return pl.pallas_call(
        expert_kernel,
        out_shape=jax.ShapeDtypeStruct(rows.shape, BF16),
        in_specs=[HBM] * 7,
        out_specs=HBM,
        scratch_shapes=[
            pltpu.VMEM(rows.shape, BF16),
            pltpu.VMEM(rows.shape, BF16),
            pltpu.VMEM((blocks, width, block), BF16),
            pltpu.VMEM((blocks, width, block), BF16),
            pltpu.VMEM((blocks, block, width), BF16),
            pltpu.VMEM((count, width), BF16),
            pltpu.VMEM((count, width), F32),
            pltpu.SemaphoreType.DMA((3, blocks)),
            pltpu.SemaphoreType.DMA((2, rows.shape[1] // 256)),
        ],
        compiler_params=pltpu.CompilerParams(vmem_limit_bytes=58 * MIB),
        cost_estimate=pl.CostEstimate(
            flops=7_500_000_000, bytes_accessed=26_000_000, transcendentals=300_000
        ),
        name="expert",
    )(rows, *far, *near)


def along_y(array, step):
    return lax.ppermute(array, "y", [(i, (i + step) % SIDE) for i in range(SIDE)])


def other_core(array):
    return lax.ppermute(array, "core", SWAP)


def shards(
    queries,
    new_latent,
    latent_cache,
    block_table,
    lengths,
    value_up,
    out_proj,
    norm_gain,
    expert_ids,
    affinity,
    gate_weight,
    up_weight,
    down_weight,
):
    seq_count = new_latent.shape[0]
    kv_width = value_up.shape[1]
    head_rows, model_width = out_proj.shape
    half = model_width // 2
    core = lax.axis_index("core")
    planes = SIDE * SIDE
    chips = SIDE**3

    piece, routes = prepare(out_proj, value_up, expert_ids, affinity)
    one, three = along_y(piece, 1), along_y(piece, -1)
    middle = head_rows // 2
    two_top, two_bottom = along_y(one[:middle], 1), along_y(three[middle:], -1)
    pieces = (piece, one, two_top, two_bottom, three)
    routes, pieces = lax.optimization_barrier((routes, pieces))
    far_routes = other_core(routes)

    latent = attend(block_table, lengths, queries, new_latent, latent_cache, kv_width)
    outbound = latent.reshape(planes, SIDE * seq_count, kv_width)
    arrived = lax.all_to_all(outbound, ("z", "x"), split_axis=0, concat_axis=0, tiled=True)
    arrived = arrived.reshape(planes * SIDE * seq_count, kv_width)
    placement, mixing = route(routes, far_routes, chips)
    own_values = find_values(arrived, pieces)
    far_values, placement, mixing = lax.optimization_barrier(
        (other_core(own_values), placement, mixing)
    )
    partial = project(own_values, far_values, pieces, half)

    partial, gate_weight = lax.optimization_barrier((partial, gate_weight))
    far_gate = other_core(gate_weight)
    partial = partial.reshape(planes, 2 * seq_count, half)
    collected = lax.all_to_all(partial, ("z", "x"), split_axis=0, concat_axis=0, tiled=True)
    collected, far_gate = lax.optimization_barrier((collected, far_gate))
    mine = jnp.sum(collected.astype(F32), axis=0)
    theirs = other_core(mine)
    theirs = jnp.concatenate([theirs[seq_count:], theirs[:seq_count]], axis=0)
    attn_out = jnp.where(
        core == 0,
        jnp.concatenate([mine, theirs], axis=1),
        jnp.concatenate([theirs, mine], axis=1),
    )
    attn_out, up_weight, down_weight = lax.optimization_barrier(
        (attn_out, up_weight, down_weight)
    )
    weights = (gate_weight, up_weight, down_weight)
    far_weights = (far_gate, other_core(up_weight), other_core(down_weight))
    mean_square = jnp.mean(attn_out * attn_out, axis=1, keepdims=True)
    both = (attn_out * lax.rsqrt(mean_square + EPSILON) * norm_gain).astype(BF16)
    normed = both[:seq_count]
    both = jnp.concatenate([both[:, :half], both[:, half:]], axis=0)
    outgoing = lax.dot_general(
        placement, both, (((0,), (0,)), ((), ())), preferred_element_type=F32
    )
    outgoing = outgoing.astype(BF16).reshape(chips, 8, half)
    received = lax.all_to_all(outgoing, CHIPS, split_axis=0, concat_axis=0, tiled=True)
    reply = run_expert(received.reshape(chips * 8, half), weights, far_weights)
    returned = lax.all_to_all(
        reply.reshape(chips, 8, half), CHIPS, split_axis=0, concat_axis=0, tiled=True
    )
    mixed = dot(mixing, returned.reshape(chips * 8, half))
    mixed = mixed[: 4 * seq_count] + mixed[4 * seq_count :]
    mixed = mixed.reshape(2, 2, seq_count, half)
    mixed = jnp.transpose(mixed, (1, 2, 0, 3)).reshape(2, seq_count, model_width)
    expert_out = (mixed[0] + other_core(mixed[1])).astype(BF16)
    return (normed, expert_out)


def solution(mesh):
    grid = Mesh(mesh.devices.reshape(2, SIDE, SIDE, SIDE), ("core",) + CHIPS)
    rows = P(("core",) + CHIPS, None)
    placed = (
        rows,
        rows,
        rows,
        rows,
        rows,
        P(CHIPS, None, None),
        P(CHIPS, None),
        P(),
        rows,
        rows,
        P(CHIPS, None, "core"),
        P(CHIPS, None, "core"),
        P(CHIPS, "core", None),
    )
    return jax.shard_map(
        shards, mesh=grid, in_specs=placed, out_specs=(rows, rows), check_vma=False
    )
```

```python
import jax
import jax.numpy as jnp
from jax import lax
from jax.experimental import pallas as pl
from jax.experimental.pallas import tpu as pltpu
from jax.sharding import Mesh, PartitionSpec as P

SCORE_SCALE = 192.0 ** (-0.5)
ROUTED_SCALE = 2.5
EPSILON = 1e-06
SIDE = 4
CHIPS = ("z", "x", "y")
PLANE = ("x", "z")
SWAP = [(0, 1), (1, 0)]
F32 = jnp.float32
BF16 = jnp.bfloat16
MIB = 1 << 20
SMEM = pl.BlockSpec(memory_space=pltpu.SMEM)
VMEM = pl.BlockSpec(memory_space=pltpu.VMEM)
HBM = pl.BlockSpec(memory_space=pltpu.HBM)


def dot_nt(a, b):
    return lax.dot_general(a, b, (((1,), (1,)), ((), ())), preferred_element_type=F32)


def dot(a, b):
    return jnp.dot(a, b, preferred_element_type=F32)


def attend_kernel(
    table_hbm, length_hbm, query_hbm, fresh_hbm, cache_hbm, out_ref,
    table_ref, length_ref, query_ref, fresh_ref, cache_ref, key_ref, sems,
):
    moves = (
        (cache_hbm, cache_ref),
        (query_hbm, query_ref),
        (table_hbm, table_ref),
        (length_hbm, length_ref),
        (fresh_hbm, fresh_ref),
    )
    copies = [pltpu.make_async_copy(a, b, sems.at[i]) for i, (a, b) in enumerate(moves)]
    for copy in copies:
        copy.start()
    seq_count, entry = fresh_ref.shape
    pages = cache_ref.shape[0]
    pairs = cache_ref.shape[1] // (2 * entry)
    wide = entry + 64
    kv_width = out_ref.shape[1]
    spots = pairs * pages
    copies[0].wait()
    for r in range(pairs):
        at = 2 * entry * r
        key_ref[0, r * pages : (r + 1) * pages, :] = cache_ref[:, at : at + wide]
        key_ref[1, r * pages : (r + 1) * pages, :] = cache_ref[:, at + entry - 64 : at + 2 * entry]
    even_keys, odd_keys = key_ref[0], key_ref[1]

    for copy in copies[1:]:
        copy.wait()
    sequence = lax.broadcasted_iota(jnp.int32, (seq_count, spots), 0)
    lane = lax.broadcasted_iota(jnp.int32, (seq_count, spots), 1)
    page, entry_at = lane % pages, 2 * (lane // pages)
    first = jnp.zeros((seq_count, spots), jnp.int32)
    second, live = first, first
    for s in range(seq_count):
        here = sequence == s
        first = jnp.where(here, table_ref[0, 2 * s], first)
        second = jnp.where(here, table_ref[0, 2 * s + 1], second)
        live = jnp.where(here, length_ref[0, s], live)

    def bias_of(position):
        inside = ((page == first) & (position < live)) | (
            (page == second) & (position + 2 * pairs < live)
        )
        return jnp.where(inside, 0.0, -jnp.inf).astype(F32)

    even_bias, odd_bias = bias_of(entry_at), bias_of(entry_at + 1)
    fresh = jnp.concatenate(
        [fresh_ref[...].astype(F32), jnp.zeros((seq_count, wide - entry), F32)], axis=1
    )
    group = 16
    for g in range(query_ref.shape[1] // (2 * entry) // group):
        base = 2 * entry * group * g
        evens = [
            query_ref[:, base + 2 * entry * i : base + 2 * entry * i + wide].astype(F32)
            for i in range(group)
        ]
        odds = [
            query_ref[:, base + 2 * entry * (i + 1) - wide : base + 2 * entry * (i + 1)].astype(F32)
            for i in range(group)
        ]
        rows = group * seq_count
        column = lax.broadcasted_iota(jnp.int32, (rows, wide), 1)
        even_low = jnp.where(column < entry, jnp.concatenate(evens, axis=0), 0.0)
        odd_high = jnp.where(column >= 64, jnp.concatenate(odds, axis=0), 0.0)
        even_high = pltpu.roll(even_low, 64, 1)
        odd_low = pltpu.roll(odd_high, entry, 1)
        low = jnp.concatenate([even_low, odd_low], axis=0)
        high = jnp.concatenate([even_high, odd_high], axis=0)
        heads = 2 * group
        own = jnp.sum(
            low.reshape(heads, seq_count, wide) * fresh[None], axis=2, keepdims=True
        ) * SCORE_SCALE
        even_scores = (dot_nt(low.astype(BF16), even_keys) * SCORE_SCALE).reshape(
            heads, seq_count, spots
        ) + even_bias[None]
        odd_scores = (dot_nt(high.astype(BF16), odd_keys) * SCORE_SCALE).reshape(
            heads, seq_count, spots
        ) + odd_bias[None]
        top = jnp.maximum(
            jnp.max(jnp.maximum(even_scores, odd_scores), axis=2, keepdims=True), own
        )
        even_raised = jnp.exp(even_scores - top)
        odd_raised = jnp.exp(odd_scores - top)
        own_raised = jnp.exp(own - top)
        scale = 1.0 / (
            jnp.sum(even_raised + odd_raised, axis=2, keepdims=True) + own_raised
        )
        even_weights = (even_raised * scale).astype(BF16).reshape(2 * rows, spots)
        odd_weights = (odd_raised * scale).astype(BF16).reshape(2 * rows, spots)
        own_weight = (own_raised * scale).astype(BF16).astype(F32)
        even_part = dot(even_weights, even_keys)[:, :kv_width]
        odd_part = pltpu.roll(dot(odd_weights, odd_keys), entry, 1)[:, :kv_width]
        own_part = (own_weight * fresh[None, :, :kv_width]).reshape(2 * rows, kv_width)
        latent = even_part + odd_part + own_part
        for i in range(group):
            two = jnp.concatenate(
                [
                    latent[i * seq_count : (i + 1) * seq_count],
                    latent[rows + i * seq_count : rows + (i + 1) * seq_count],
                ],
                axis=0,
            )
            head = 2 * (group * g + i)
            across, along, within = head // SIDE**2, head // SIDE % SIDE, head % SIDE
            at = seq_count * ((along * SIDE + across) * SIDE + within)
            out_ref[at : at + 2 * seq_count, :] = two.astype(BF16)


def attend(block_table, lengths, queries, new_latent, latent_cache, kv_width):
    seq_count, entry = new_latent.shape
    head_count = queries.shape[1] // entry
    pages, page_width = latent_cache.shape
    spots = pages * page_width // (2 * entry)
    return pl.pallas_call(
        attend_kernel,
        out_shape=jax.ShapeDtypeStruct((head_count * seq_count, kv_width), BF16),
        in_specs=[HBM] * 5,
        out_specs=VMEM,
        scratch_shapes=[
            pltpu.SMEM(block_table.shape, jnp.int32),
            pltpu.SMEM(lengths.shape, jnp.int32),
            pltpu.VMEM(queries.shape, BF16),
            pltpu.VMEM(new_latent.shape, BF16),
            pltpu.VMEM(latent_cache.shape, BF16),
            pltpu.VMEM((2, spots, entry + 64), BF16),
            pltpu.SemaphoreType.DMA((5,)),
        ],
        compiler_params=pltpu.CompilerParams(vmem_limit_bytes=60 * MIB),
        cost_estimate=pl.CostEstimate(
            flops=1_400_000_000, bytes_accessed=2_400_000, transcendentals=600_000
        ),
        name="attend",
    )(block_table, lengths, queries, new_latent, latent_cache)


def prepare_kernel(out_proj, value_up, ids_hbm, affinity_hbm, piece, routes, ids, affinity, sems):
    core = lax.axis_index("core")
    head_rows, half = out_proj.shape[0], out_proj.shape[1] // 2
    at = pl.ds(pl.multiple_of(core * half, 128), half)
    moves = [
        (ids_hbm, ids),
        (affinity_hbm, affinity),
        (out_proj.at[:, at], piece.at[:, :half]),
    ]
    for b in range(value_up.shape[1] // head_rows):
        rows = pl.ds(b * head_rows, head_rows)
        columns = pl.ds(half + b * head_rows, head_rows)
        moves.append((value_up.at[0, rows], piece.at[:, columns]))
    copies = [pltpu.make_async_copy(a, b, sems.at[i]) for i, (a, b) in enumerate(moves)]
    for copy in copies:
        copy.start()
    for copy in copies[:2]:
        copy.wait()
    rows, top_count = ids.shape
    rest = jnp.zeros((rows, routes.shape[1] - 2 * top_count), F32)
    routes[...] = jnp.concatenate([ids[...].astype(F32), affinity[...], rest], axis=1)
    for copy in copies[2:]:
        copy.wait()


def prepare(out_proj, value_up, expert_ids, affinity):
    head_rows, width = out_proj.shape
    return pl.pallas_call(
        prepare_kernel,
        out_shape=(
            jax.ShapeDtypeStruct((head_rows, width // 2 + value_up.shape[1]), BF16),
            jax.ShapeDtypeStruct((expert_ids.shape[0], 128), F32),
        ),
        in_specs=[HBM] * 4,
        out_specs=(VMEM, VMEM),
        scratch_shapes=[
            pltpu.VMEM(expert_ids.shape, jnp.int32),
            pltpu.VMEM(affinity.shape, F32),
            pltpu.SemaphoreType.DMA((3 + value_up.shape[1] // head_rows,)),
        ],
        compiler_params=pltpu.CompilerParams(vmem_limit_bytes=60 * MIB),
        cost_estimate=pl.CostEstimate(flops=0, bytes_accessed=1_200_000, transcendentals=0),
        name="prepare",
    )(out_proj, value_up, expert_ids, affinity)


def route_kernel(own_ref, far_ref, place_ref, mix_ref):
    core = lax.axis_index("core")
    seq_count = own_ref.shape[0]
    tokens, top_count = 2 * seq_count, 8
    columns = place_ref.shape[1]
    routes = jnp.concatenate([own_ref[...], far_ref[...]], axis=0)
    affinity = routes[:, top_count : 2 * top_count]
    share = affinity / jnp.sum(affinity, axis=1, keepdims=True) * ROUTED_SCALE
    experts = routes.shape[1]
    expert = lax.broadcasted_iota(jnp.int32, (tokens, experts), 1).astype(F32)
    chosen = jnp.zeros((tokens, experts), F32)
    shares = jnp.zeros((tokens, experts), F32)
    for k in range(top_count):
        hit = expert == routes[:, k : k + 1]
        chosen = jnp.where(hit, 1.0, chosen)
        shares = jnp.where(hit, share[:, k : k + 1], shares)
    row = lax.broadcasted_iota(jnp.int32, (tokens, tokens), 0)
    column = lax.broadcasted_iota(jnp.int32, (tokens, tokens), 1)
    earlier = ((column < row) & (column // seq_count == row // seq_count)).astype(F32)
    rank = dot(earlier.astype(BF16), chosen.astype(BF16))
    token = lax.broadcasted_iota(jnp.int32, (tokens, experts), 0)
    slot = (rank + jnp.where(token < seq_count, 1.0, 3.0)) * chosen
    named = lax.broadcasted_iota(jnp.int32, (experts, columns), 0)
    at = lax.broadcasted_iota(jnp.int32, (experts, columns), 1)
    spread = (named == at // 8 * 2 + core).astype(F32).astype(BF16)
    high = shares.astype(BF16)
    low = (shares - high.astype(F32)).astype(BF16)
    at = lax.broadcasted_iota(jnp.int32, (tokens, columns), 1)
    filled = dot(slot.astype(BF16), spread) == (at % 4 + 1).astype(F32)
    high = jnp.where(filled, dot(high, spread), 0.0)
    low = jnp.where(filled, dot(low, spread), 0.0)
    placed = filled.astype(F32)
    first = at % 8 < 4

    def by_half(table):
        return [jnp.where(first, table, 0.0), jnp.where(first, 0.0, table)]

    place_ref[...] = jnp.concatenate(by_half(placed), axis=0).astype(BF16)
    mix_ref[...] = jnp.concatenate(by_half(high) + by_half(low), axis=0).astype(BF16)


def route(own, far, chips):
    tokens = 2 * own.shape[0]
    return pl.pallas_call(
        route_kernel,
        out_shape=(
            jax.ShapeDtypeStruct((2 * tokens, chips * 8), BF16),
            jax.ShapeDtypeStruct((4 * tokens, chips * 8), BF16),
        ),
        in_specs=[VMEM] * 2,
        out_specs=(VMEM, VMEM),
        compiler_params=pltpu.CompilerParams(vmem_limit_bytes=8 * MIB),
        cost_estimate=pl.CostEstimate(
            flops=20_000_000, bytes_accessed=120_000, transcendentals=0
        ),
        name="route",
    )(own, far)


def value_kernel(arrived_ref, *refs):
    *piece_refs, out_ref = refs
    place_y = lax.axis_index("y")
    rows, kv_width = arrived_ref.shape
    tokens = rows // SIDE
    head_rows = piece_refs[0].shape[0]
    half = piece_refs[0].shape[1] - kv_width
    to = lax.broadcasted_iota(jnp.int32, (tokens, rows), 0)
    source = lax.broadcasted_iota(jnp.int32, (tokens, rows), 1)
    plane, seq = to // 8, to % 8
    arrived = arrived_ref[...]
    own, one, top, bottom, three = piece_refs
    for k in range(SIDE):
        head = lax.rem(place_y - k + SIDE, SIDE)
        pick = (source == plane * (SIDE * 8) + head * 8 + seq).astype(F32)
        latent = dot(pick.astype(BF16), arrived).astype(BF16)
        total = jnp.zeros((tokens, head_rows), F32)
        for at in range(0, kv_width, head_rows):
            columns = slice(half + at, half + at + head_rows)
            if k == 2:
                up = jnp.concatenate([top[:, columns], bottom[:, columns]], axis=0)
            else:
                up = (own, one, None, three)[k][:, columns]
            total = total + dot(latent[:, at : at + head_rows], up)
        out_ref[:, k * head_rows : (k + 1) * head_rows] = total.astype(BF16)


def find_values(arrived, pieces):
    rows = arrived.shape[0]
    return pl.pallas_call(
        value_kernel,
        out_shape=jax.ShapeDtypeStruct((rows // SIDE, SIDE * pieces[0].shape[0]), BF16),
        in_specs=[VMEM] * 6,
        out_specs=VMEM,
        compiler_params=pltpu.CompilerParams(vmem_limit_bytes=12 * MIB),
        cost_estimate=pl.CostEstimate(
            flops=350_000_000, bytes_accessed=3_200_000, transcendentals=0
        ),
        name="find_values",
    )(arrived, *pieces)


def project_kernel(own_values, far_values, *refs):
    own, one, top, bottom, three, out_ref = refs
    rows = own_values.shape[0]
    half = out_ref.shape[1]
    to = lax.broadcasted_iota(jnp.int32, (2 * rows, rows), 0)
    source = lax.broadcasted_iota(jnp.int32, (2 * rows, rows), 1)
    same = source == to // 16 * 8 + to % 8
    near = (same & (to % 16 < 8)).astype(F32).astype(BF16)
    far = (same & (to % 16 >= 8)).astype(F32).astype(BF16)
    values = (dot(near, own_values[...]) + dot(far, far_values[...])).astype(BF16)
    step = 256
    for at in range(0, half, step):
        columns = slice(at, at + step)
        part = jnp.concatenate([ref[:, columns] for ref in (own, one, top, bottom, three)], axis=0)
        out_ref[:, columns] = dot(values, part).astype(BF16)


def project(own_values, far_values, pieces, half):
    return pl.pallas_call(
        project_kernel,
        out_shape=jax.ShapeDtypeStruct((2 * own_values.shape[0], half), BF16),
        in_specs=[VMEM] * 7,
        out_specs=VMEM,
        compiler_params=pltpu.CompilerParams(vmem_limit_bytes=12 * MIB),
        cost_estimate=pl.CostEstimate(
            flops=600_000_000, bytes_accessed=3_000_000, transcendentals=0
        ),
        name="project",
    )(own_values, far_values, *pieces)


def expert_kernel(
    rows_ref, gate_far, up_far, down_far, gate_near, up_near, down_near, out_ref,
    gate_buf, up_buf, down_buf, wide_ref, total_ref, sems,
):
    core = lax.axis_index("core")
    blocks, width, block = gate_buf.shape
    half = width // 2
    count = total_ref.shape[0]

    def copies(i):
        near = i >= blocks // 2
        gate, up, down = (gate_near, up_near, down_near) if near else (gate_far, up_far, down_far)
        at = pl.ds((i % (blocks // 2)) * block, block)
        return (
            pltpu.make_async_copy(gate.at[core, :, at], gate_buf.at[i], sems.at[0, i]),
            pltpu.make_async_copy(up.at[core, :, at], up_buf.at[i], sems.at[1, i]),
            pltpu.make_async_copy(down.at[core, at, :], down_buf.at[i], sems.at[2, i]),
        )

    step = 256
    started = [copies(i) for i in range(blocks)]
    for copy in started[0]:
        copy.start()

    to = lax.broadcasted_iota(jnp.int32, (count, 2 * count), 0)
    source = lax.broadcasted_iota(jnp.int32, (count, 2 * count), 1)
    picks = [
        (source == to // 4 * 8 + to % 4 + 4 * side).astype(F32).astype(BF16) for side in range(2)
    ]
    for side in range(2):
        for at in range(0, half, step):
            wide_ref[:, side * half + at : side * half + at + step] = dot(
                picks[side], rows_ref[:, at : at + step]
            ).astype(BF16)

    for copy in started[1]:
        copy.start()

    for i in range(blocks):
        started[i][0].wait()
        started[i][1].wait()
        if i + 2 < blocks:
            for copy in started[i + 2]:
                copy.start()
        gate = dot(wide_ref[...], gate_buf[i])
        up = dot(wide_ref[...], up_buf[i])
        hidden = (gate / (1.0 + jnp.exp(-gate)) * up).astype(BF16)
        started[i][2].wait()
        for at in range(0, width, 2 * step):
            part = dot(hidden, down_buf[i, :, at : at + 2 * step])
            if i == 0:
                total_ref[:, at : at + 2 * step] = part
            else:
                total_ref[:, at : at + 2 * step] += part

    to = lax.broadcasted_iota(jnp.int32, (2 * count, count), 0)
    source = lax.broadcasted_iota(jnp.int32, (2 * count, count), 1)
    same = source == to // 8 * 4 + to % 4
    first = ((to % 8 < 4) & same).astype(F32).astype(BF16)
    second = ((to % 8 >= 4) & same).astype(F32).astype(BF16)
    for at in range(0, half, step):
        out_ref[:, at : at + step] = (
            dot(first, total_ref[:, at : at + step].astype(BF16))
            + dot(second, total_ref[:, half + at : half + at + step].astype(BF16))
        ).astype(BF16)


def run_expert(rows, near, far):
    _, hidden, width = near[2].shape
    count, block = rows.shape[0] // 2, 256
    blocks = 2 * hidden // block
    return pl.pallas_call(
        expert_kernel,
        out_shape=jax.ShapeDtypeStruct(rows.shape, BF16),
        in_specs=[VMEM] + [HBM] * 6,
        out_specs=VMEM,
        scratch_shapes=[
            pltpu.VMEM((blocks, width, block), BF16),
            pltpu.VMEM((blocks, width, block), BF16),
            pltpu.VMEM((blocks, block, width), BF16),
            pltpu.VMEM((count, width), BF16),
            pltpu.VMEM((count, width), F32),
            pltpu.SemaphoreType.DMA((3, blocks)),
        ],
        compiler_params=pltpu.CompilerParams(vmem_limit_bytes=29 * MIB),
        cost_estimate=pl.CostEstimate(
            flops=7_500_000_000, bytes_accessed=26_000_000, transcendentals=300_000
        ),
        name="expert",
    )(rows, *far, *near)


def along_y(array, step):
    return lax.ppermute(array, "y", [(i, (i + step) % SIDE) for i in range(SIDE)])


def other_core(array):
    return lax.ppermute(array, "core", SWAP)


def shards(
    queries,
    new_latent,
    latent_cache,
    block_table,
    lengths,
    value_up,
    out_proj,
    norm_gain,
    expert_ids,
    affinity,
    gate_weight,
    up_weight,
    down_weight,
):
    seq_count = new_latent.shape[0]
    kv_width = value_up.shape[1]
    head_rows, model_width = out_proj.shape
    half = model_width // 2
    core = lax.axis_index("core")
    planes = SIDE * SIDE
    chips = SIDE**3

    piece, routes = prepare(out_proj, value_up, expert_ids, affinity)
    one, three = along_y(piece, 1), along_y(piece, -1)
    middle = head_rows // 2
    two_top, two_bottom = along_y(one[:middle], 1), along_y(three[middle:], -1)
    pieces = (piece, one, two_top, two_bottom, three)
    routes, pieces = lax.optimization_barrier((routes, pieces))
    far_routes = other_core(routes)

    latent = attend(block_table, lengths, queries, new_latent, latent_cache, kv_width)
    outbound = latent.reshape(planes, SIDE * seq_count, kv_width)
    arrived = lax.all_to_all(outbound, PLANE, split_axis=0, concat_axis=0, tiled=True)
    arrived = arrived.reshape(planes * SIDE * seq_count, kv_width)
    placement, mixing = route(routes, far_routes, chips)
    own_values = find_values(arrived, pieces)
    far_values, placement, mixing = lax.optimization_barrier(
        (other_core(own_values), placement, mixing)
    )
    partial = project(own_values, far_values, pieces, half)

    partial, gate_weight = lax.optimization_barrier((partial, gate_weight))
    far_gate = other_core(gate_weight)
    partial = partial.reshape(planes, 2 * seq_count, half)
    collected = lax.all_to_all(partial, PLANE, split_axis=0, concat_axis=0, tiled=True)
    mine = jnp.sum(collected.astype(F32), axis=0)
    theirs = other_core(mine)
    theirs = jnp.concatenate([theirs[seq_count:], theirs[:seq_count]], axis=0)
    attn_out = jnp.where(
        core == 0,
        jnp.concatenate([mine, theirs], axis=1),
        jnp.concatenate([theirs, mine], axis=1),
    )
    attn_out, up_weight, down_weight = lax.optimization_barrier(
        (attn_out, up_weight, down_weight)
    )
    weights = (gate_weight, up_weight, down_weight)
    far_weights = (far_gate, other_core(up_weight), other_core(down_weight))
    mean_square = jnp.mean(attn_out * attn_out, axis=1, keepdims=True)
    both = (attn_out * lax.rsqrt(mean_square + EPSILON) * norm_gain).astype(BF16)
    normed = both[:seq_count]
    both = jnp.concatenate([both[:, :half], both[:, half:]], axis=0)
    outgoing = lax.dot_general(
        placement, both, (((0,), (0,)), ((), ())), preferred_element_type=F32
    )
    outgoing = outgoing.astype(BF16).reshape(chips, 8, half)
    received = lax.all_to_all(outgoing, CHIPS, split_axis=0, concat_axis=0, tiled=True)
    reply = run_expert(received.reshape(chips * 8, half), weights, far_weights)
    returned = lax.all_to_all(
        reply.reshape(chips, 8, half), CHIPS, split_axis=0, concat_axis=0, tiled=True
    )
    mixed = dot(mixing, returned.reshape(chips * 8, half))
    mixed = mixed[: 4 * seq_count] + mixed[4 * seq_count :]
    mixed = mixed.reshape(2, 2, seq_count, half)
    mixed = jnp.transpose(mixed, (1, 2, 0, 3)).reshape(2, seq_count, model_width)
    expert_out = (mixed[0] + other_core(mixed[1])).astype(BF16)
    return (normed, expert_out)


def solution(mesh):
    grid = Mesh(mesh.devices.reshape(2, SIDE, SIDE, SIDE), ("core",) + CHIPS)
    rows = P(("core",) + CHIPS, None)
    placed = (
        rows,
        rows,
        rows,
        rows,
        rows,
        P(CHIPS, None, None),
        P(CHIPS, None),
        P(),
        rows,
        rows,
        P(CHIPS, None, "core"),
        P(CHIPS, None, "core"),
        P(CHIPS, "core", None),
    )
    return jax.shard_map(
        shards, mesh=grid, in_specs=placed, out_specs=(rows, rows), check_vma=False
    )
```

```python
import jax
import jax.numpy as jnp
from jax import lax
from jax.experimental import pallas as pl
from jax.experimental.pallas import tpu as pltpu
from jax.sharding import Mesh, PartitionSpec as P

SCORE_SCALE = 192.0 ** (-0.5)
ROUTED_SCALE = 2.5
EPSILON = 1e-06
SIDE = 4
CHIPS = ("z", "x", "y")
PLANE = ("x", "z")
ALL = ("core",) + CHIPS
SWAP = [(0, 1), (1, 0)]
F32 = jnp.float32
BF16 = jnp.bfloat16
MIB = 1 << 20
SMEM = pl.BlockSpec(memory_space=pltpu.SMEM)
VMEM = pl.BlockSpec(memory_space=pltpu.VMEM)
HBM = pl.BlockSpec(memory_space=pltpu.HBM)


def dot_nt(a, b):
    return lax.dot_general(a, b, (((1,), (1,)), ((), ())), preferred_element_type=F32)


def dot(a, b):
    return jnp.dot(a, b, preferred_element_type=F32)


def attend_kernel(
    table_hbm, length_hbm, query_hbm, fresh_hbm, cache_hbm, out_ref,
    table_ref, length_ref, query_ref, fresh_ref, cache_ref, key_ref, sems,
):
    moves = (
        (cache_hbm, cache_ref),
        (query_hbm, query_ref),
        (table_hbm, table_ref),
        (length_hbm, length_ref),
        (fresh_hbm, fresh_ref),
    )
    copies = [pltpu.make_async_copy(a, b, sems.at[i]) for i, (a, b) in enumerate(moves)]
    for copy in copies:
        copy.start()
    seq_count, entry = fresh_ref.shape
    pages = cache_ref.shape[0]
    pairs = cache_ref.shape[1] // (2 * entry)
    wide = entry + 64
    kv_width = out_ref.shape[1]
    spots = pairs * pages
    copies[0].wait()
    for r in range(pairs):
        at = 2 * entry * r
        key_ref[0, r * pages : (r + 1) * pages, :] = cache_ref[:, at : at + wide]
        key_ref[1, r * pages : (r + 1) * pages, :] = cache_ref[:, at + entry - 64 : at + 2 * entry]
    even_keys, odd_keys = key_ref[0], key_ref[1]

    for copy in copies[1:]:
        copy.wait()
    sequence = lax.broadcasted_iota(jnp.int32, (seq_count, spots), 0)
    lane = lax.broadcasted_iota(jnp.int32, (seq_count, spots), 1)
    page, entry_at = lane % pages, 2 * (lane // pages)
    first = jnp.zeros((seq_count, spots), jnp.int32)
    second, live = first, first
    for s in range(seq_count):
        here = sequence == s
        first = jnp.where(here, table_ref[0, 2 * s], first)
        second = jnp.where(here, table_ref[0, 2 * s + 1], second)
        live = jnp.where(here, length_ref[0, s], live)

    def bias_of(position):
        inside = ((page == first) & (position < live)) | (
            (page == second) & (position + 2 * pairs < live)
        )
        return jnp.where(inside, 0.0, -jnp.inf).astype(F32)

    even_bias, odd_bias = bias_of(entry_at), bias_of(entry_at + 1)
    fresh = jnp.concatenate(
        [fresh_ref[...].astype(F32), jnp.zeros((seq_count, wide - entry), F32)], axis=1
    )
    group = 16
    for g in range(query_ref.shape[1] // (2 * entry) // group):
        base = 2 * entry * group * g
        evens = [
            query_ref[:, base + 2 * entry * i : base + 2 * entry * i + wide].astype(F32)
            for i in range(group)
        ]
        odds = [
            query_ref[:, base + 2 * entry * (i + 1) - wide : base + 2 * entry * (i + 1)].astype(F32)
            for i in range(group)
        ]
        rows = group * seq_count
        column = lax.broadcasted_iota(jnp.int32, (rows, wide), 1)
        even_low = jnp.where(column < entry, jnp.concatenate(evens, axis=0), 0.0)
        odd_high = jnp.where(column >= 64, jnp.concatenate(odds, axis=0), 0.0)
        even_high = pltpu.roll(even_low, 64, 1)
        odd_low = pltpu.roll(odd_high, entry, 1)
        low = jnp.concatenate([even_low, odd_low], axis=0)
        high = jnp.concatenate([even_high, odd_high], axis=0)
        heads = 2 * group
        own = jnp.sum(
            low.reshape(heads, seq_count, wide) * fresh[None], axis=2, keepdims=True
        ) * SCORE_SCALE
        even_scores = (dot_nt(low.astype(BF16), even_keys) * SCORE_SCALE).reshape(
            heads, seq_count, spots
        ) + even_bias[None]
        odd_scores = (dot_nt(high.astype(BF16), odd_keys) * SCORE_SCALE).reshape(
            heads, seq_count, spots
        ) + odd_bias[None]
        top = jnp.maximum(
            jnp.max(jnp.maximum(even_scores, odd_scores), axis=2, keepdims=True), own
        )
        even_raised = jnp.exp(even_scores - top)
        odd_raised = jnp.exp(odd_scores - top)
        own_raised = jnp.exp(own - top)
        scale = 1.0 / (
            jnp.sum(even_raised + odd_raised, axis=2, keepdims=True) + own_raised
        )
        even_weights = (even_raised * scale).astype(BF16).reshape(2 * rows, spots)
        odd_weights = (odd_raised * scale).astype(BF16).reshape(2 * rows, spots)
        own_weight = (own_raised * scale).astype(BF16).astype(F32)
        even_part = dot(even_weights, even_keys)[:, :kv_width]
        odd_part = pltpu.roll(dot(odd_weights, odd_keys), entry, 1)[:, :kv_width]
        own_part = (own_weight * fresh[None, :, :kv_width]).reshape(2 * rows, kv_width)
        latent = even_part + odd_part + own_part
        for i in range(group):
            two = jnp.concatenate(
                [
                    latent[i * seq_count : (i + 1) * seq_count],
                    latent[rows + i * seq_count : rows + (i + 1) * seq_count],
                ],
                axis=0,
            )
            head = 2 * (group * g + i)
            across, along, within = head // SIDE**2, head // SIDE % SIDE, head % SIDE
            at = seq_count * ((along * SIDE + across) * SIDE + within)
            out_ref[at : at + 2 * seq_count, :] = two.astype(BF16)


def attend(block_table, lengths, queries, new_latent, latent_cache, kv_width):
    seq_count, entry = new_latent.shape
    head_count = queries.shape[1] // entry
    pages, page_width = latent_cache.shape
    spots = pages * page_width // (2 * entry)
    return pl.pallas_call(
        attend_kernel,
        out_shape=jax.ShapeDtypeStruct((head_count * seq_count, kv_width), BF16),
        in_specs=[HBM] * 5,
        out_specs=VMEM,
        scratch_shapes=[
            pltpu.SMEM(block_table.shape, jnp.int32),
            pltpu.SMEM(lengths.shape, jnp.int32),
            pltpu.VMEM(queries.shape, BF16),
            pltpu.VMEM(new_latent.shape, BF16),
            pltpu.VMEM(latent_cache.shape, BF16),
            pltpu.VMEM((2, spots, entry + 64), BF16),
            pltpu.SemaphoreType.DMA((5,)),
        ],
        compiler_params=pltpu.CompilerParams(vmem_limit_bytes=60 * MIB),
        cost_estimate=pl.CostEstimate(
            flops=1_400_000_000, bytes_accessed=2_400_000, transcendentals=600_000
        ),
        name="attend",
    )(block_table, lengths, queries, new_latent, latent_cache)


def prepare_kernel(out_proj, value_up, ids_hbm, affinity_hbm, piece, routes, ids, affinity, sems):
    core = lax.axis_index("core")
    head_rows, half = out_proj.shape[0], out_proj.shape[1] // 2
    at = pl.ds(pl.multiple_of(core * half, 128), half)
    moves = [
        (ids_hbm, ids),
        (affinity_hbm, affinity),
        (out_proj.at[:, at], piece.at[:, :half]),
    ]
    for b in range(value_up.shape[1] // head_rows):
        rows = pl.ds(b * head_rows, head_rows)
        columns = pl.ds(half + b * head_rows, head_rows)
        moves.append((value_up.at[0, rows], piece.at[:, columns]))
    copies = [pltpu.make_async_copy(a, b, sems.at[i]) for i, (a, b) in enumerate(moves)]
    for copy in copies:
        copy.start()
    for copy in copies[:2]:
        copy.wait()
    rows, top_count = ids.shape
    rest = jnp.zeros((rows, routes.shape[1] - 2 * top_count), F32)
    routes[...] = jnp.concatenate([ids[...].astype(F32), affinity[...], rest], axis=1)
    for copy in copies[2:]:
        copy.wait()


def prepare(out_proj, value_up, expert_ids, affinity):
    head_rows, width = out_proj.shape
    return pl.pallas_call(
        prepare_kernel,
        out_shape=(
            jax.ShapeDtypeStruct((head_rows, width // 2 + value_up.shape[1]), BF16),
            jax.ShapeDtypeStruct((expert_ids.shape[0], 128), F32),
        ),
        in_specs=[HBM] * 4,
        out_specs=(VMEM, VMEM),
        scratch_shapes=[
            pltpu.VMEM(expert_ids.shape, jnp.int32),
            pltpu.VMEM(affinity.shape, F32),
            pltpu.SemaphoreType.DMA((3 + value_up.shape[1] // head_rows,)),
        ],
        compiler_params=pltpu.CompilerParams(vmem_limit_bytes=60 * MIB),
        cost_estimate=pl.CostEstimate(flops=0, bytes_accessed=1_200_000, transcendentals=0),
        name="prepare",
    )(out_proj, value_up, expert_ids, affinity)


def route_kernel(own_ref, place_ref, mix_ref):
    own, top_count = own_ref.shape[0], 8
    tokens = 2 * own
    columns = place_ref.shape[1]
    routes = jnp.concatenate([own_ref[...], own_ref[...]], axis=0)
    affinity = routes[:, top_count : 2 * top_count]
    share = affinity / jnp.sum(affinity, axis=1, keepdims=True) * ROUTED_SCALE
    experts = routes.shape[1]
    expert = lax.broadcasted_iota(jnp.int32, (tokens, experts), 1).astype(F32)
    chosen = jnp.zeros((tokens, experts), F32)
    shares = jnp.zeros((tokens, experts), F32)
    for k in range(top_count):
        hit = expert == routes[:, k : k + 1]
        chosen = jnp.where(hit, 1.0, chosen)
        shares = jnp.where(hit, share[:, k : k + 1], shares)
    row = lax.broadcasted_iota(jnp.int32, (tokens, tokens), 0)
    column = lax.broadcasted_iota(jnp.int32, (tokens, tokens), 1)
    earlier = ((column < row) & (column // own == row // own)).astype(F32)
    rank = dot(earlier.astype(BF16), chosen.astype(BF16))
    slot = (rank + 1.0) * chosen
    named = lax.broadcasted_iota(jnp.int32, (experts, columns), 0)
    at = lax.broadcasted_iota(jnp.int32, (experts, columns), 1)
    each = columns // 2
    spread = (named == at % each // 8 * 2 + at // each).astype(F32).astype(BF16)
    high = shares.astype(BF16)
    low = (shares - high.astype(F32)).astype(BF16)
    at = lax.broadcasted_iota(jnp.int32, (tokens, columns), 1)
    filled = dot(slot.astype(BF16), spread) == (at % 2 + 1).astype(F32)
    high = jnp.where(filled, dot(high, spread), 0.0)
    low = jnp.where(filled, dot(low, spread), 0.0)
    placed = filled.astype(F32)
    quarter = at % 8 // 2

    def by_quarter(table):
        return [jnp.where(quarter == q, table, 0.0)[:own] for q in range(4)]

    place_ref[...] = jnp.concatenate(by_quarter(placed), axis=0).astype(BF16)
    mix_ref[...] = jnp.concatenate(by_quarter(high) + by_quarter(low), axis=0).astype(BF16)


def route(own, devices):
    rows = 4 * own.shape[0]
    return pl.pallas_call(
        route_kernel,
        out_shape=(
            jax.ShapeDtypeStruct((rows, devices * 8), BF16),
            jax.ShapeDtypeStruct((2 * rows, devices * 8), BF16),
        ),
        in_specs=[VMEM],
        out_specs=(VMEM, VMEM),
        compiler_params=pltpu.CompilerParams(vmem_limit_bytes=8 * MIB),
        cost_estimate=pl.CostEstimate(
            flops=20_000_000, bytes_accessed=220_000, transcendentals=0
        ),
        name="route",
    )(own)


def value_kernel(arrived_ref, *refs):
    *piece_refs, out_ref = refs
    place_y = lax.axis_index("y")
    rows, kv_width = arrived_ref.shape
    tokens = rows // SIDE
    head_rows = piece_refs[0].shape[0]
    half = piece_refs[0].shape[1] - kv_width
    to = lax.broadcasted_iota(jnp.int32, (tokens, rows), 0)
    source = lax.broadcasted_iota(jnp.int32, (tokens, rows), 1)
    plane, seq = to // 8, to % 8
    arrived = arrived_ref[...]
    own, one, top, bottom, three = piece_refs
    for k in range(SIDE):
        head = lax.rem(place_y - k + SIDE, SIDE)
        pick = (source == plane * (SIDE * 8) + head * 8 + seq).astype(F32)
        latent = dot(pick.astype(BF16), arrived).astype(BF16)
        total = jnp.zeros((tokens, head_rows), F32)
        for at in range(0, kv_width, head_rows):
            columns = slice(half + at, half + at + head_rows)
            if k == 2:
                up = jnp.concatenate([top[:, columns], bottom[:, columns]], axis=0)
            else:
                up = (own, one, None, three)[k][:, columns]
            total = total + dot(latent[:, at : at + head_rows], up)
        out_ref[:, k * head_rows : (k + 1) * head_rows] = total.astype(BF16)


def find_values(arrived, pieces):
    rows = arrived.shape[0]
    return pl.pallas_call(
        value_kernel,
        out_shape=jax.ShapeDtypeStruct((rows // SIDE, SIDE * pieces[0].shape[0]), BF16),
        in_specs=[VMEM] * 6,
        out_specs=VMEM,
        compiler_params=pltpu.CompilerParams(vmem_limit_bytes=12 * MIB),
        cost_estimate=pl.CostEstimate(
            flops=350_000_000, bytes_accessed=3_200_000, transcendentals=0
        ),
        name="find_values",
    )(arrived, *pieces)


def project_kernel(own_values, far_values, own, one, top, bottom, three, out_ref):
    core = lax.axis_index("core")
    rows, half = own_values.shape[0], out_ref.shape[1]
    mine, theirs = own_values[...].astype(F32), far_values[...].astype(F32)
    values = jnp.concatenate(
        [jnp.where(core == 0, mine, theirs), jnp.where(core == 0, theirs, mine)], axis=0
    ).astype(BF16)
    step = 256
    for at in range(0, half, step):
        columns = slice(at, at + step)
        part = jnp.concatenate([ref[:, columns] for ref in (own, one, top, bottom, three)], axis=0)
        out_ref[:, columns] = dot(values, part).astype(BF16)


def project(own_values, far_values, pieces, half):
    return pl.pallas_call(
        project_kernel,
        out_shape=jax.ShapeDtypeStruct((2 * own_values.shape[0], half), BF16),
        in_specs=[VMEM] * 7,
        out_specs=VMEM,
        compiler_params=pltpu.CompilerParams(vmem_limit_bytes=12 * MIB),
        cost_estimate=pl.CostEstimate(
            flops=600_000_000, bytes_accessed=3_000_000, transcendentals=0
        ),
        name="project",
    )(own_values, far_values, *pieces)


def expert_kernel(
    rows_ref, gate_far, up_far, down_far, gate_near, up_near, down_near, out_ref,
    gate_buf, up_buf, down_buf, wide_ref, total_ref, sems,
):
    core = lax.axis_index("core")
    blocks, width, block = gate_buf.shape
    quarter = width // 4
    count = total_ref.shape[0]

    def copies(i):
        near = i >= blocks // 2
        gate, up, down = (gate_near, up_near, down_near) if near else (gate_far, up_far, down_far)
        at = pl.ds((i % (blocks // 2)) * block, block)
        return (
            pltpu.make_async_copy(gate.at[core, :, at], gate_buf.at[i], sems.at[0, i]),
            pltpu.make_async_copy(up.at[core, :, at], up_buf.at[i], sems.at[1, i]),
            pltpu.make_async_copy(down.at[core, at, :], down_buf.at[i], sems.at[2, i]),
        )

    step = 256
    started = [copies(i) for i in range(blocks)]
    for copy in started[0]:
        copy.start()

    sent = lax.broadcasted_iota(jnp.int32, (256, 256), 1)
    whole = lax.broadcasted_iota(jnp.int32, (256, 256), 0)
    gather = sent == whole % 64 // 2 * 8 + whole // 64 * 2 + whole % 2
    gather = gather.astype(F32).astype(BF16)
    for g in range(count // 64):
        held = dot(gather, rows_ref[g * 256 : (g + 1) * 256, :]).astype(BF16)
        for q in range(4):
            wide_ref[g * 64 : (g + 1) * 64, q * quarter : (q + 1) * quarter] = held[
                q * 64 : (q + 1) * 64
            ]

    for copy in started[1]:
        copy.start()

    for i in range(blocks):
        started[i][0].wait()
        started[i][1].wait()
        if i + 2 < blocks:
            for copy in started[i + 2]:
                copy.start()
        gate = dot(wide_ref[...], gate_buf[i])
        up = dot(wide_ref[...], up_buf[i])
        hidden = (gate / (1.0 + jnp.exp(-gate)) * up).astype(BF16)
        started[i][2].wait()
        for at in range(0, width, 2 * step):
            part = dot(hidden, down_buf[i, :, at : at + 2 * step])
            if i == 0:
                total_ref[:, at : at + 2 * step] = part
            else:
                total_ref[:, at : at + 2 * step] += part

    sent = lax.broadcasted_iota(jnp.int32, (256, 256), 0)
    whole = lax.broadcasted_iota(jnp.int32, (256, 256), 1)
    scatter = sent == whole % 64 // 2 * 8 + whole // 64 * 2 + whole % 2
    scatter = scatter.astype(F32).astype(BF16)
    for g in range(count // 64):
        held = [
            total_ref[g * 64 : (g + 1) * 64, q * quarter : (q + 1) * quarter].astype(BF16)
            for q in range(4)
        ]
        out_ref[g * 256 : (g + 1) * 256, :] = dot(
            scatter, jnp.concatenate(held, axis=0)
        ).astype(BF16)


def run_expert(rows, near, far):
    _, hidden, width = near[2].shape
    count, block = rows.shape[0] // 4, 256
    blocks = 2 * hidden // block
    return pl.pallas_call(
        expert_kernel,
        out_shape=jax.ShapeDtypeStruct(rows.shape, BF16),
        in_specs=[VMEM] + [HBM] * 6,
        out_specs=VMEM,
        scratch_shapes=[
            pltpu.VMEM((blocks, width, block), BF16),
            pltpu.VMEM((blocks, width, block), BF16),
            pltpu.VMEM((blocks, block, width), BF16),
            pltpu.VMEM((count, width), BF16),
            pltpu.VMEM((count, width), F32),
            pltpu.SemaphoreType.DMA((3, blocks)),
        ],
        compiler_params=pltpu.CompilerParams(vmem_limit_bytes=29 * MIB),
        cost_estimate=pl.CostEstimate(
            flops=7_500_000_000, bytes_accessed=26_000_000, transcendentals=300_000
        ),
        name="expert",
    )(rows, *far, *near)


def along_y(array, step):
    return lax.ppermute(array, "y", [(i, (i + step) % SIDE) for i in range(SIDE)])


def other_core(array):
    return lax.ppermute(array, "core", SWAP)


def shards(
    queries,
    new_latent,
    latent_cache,
    block_table,
    lengths,
    value_up,
    out_proj,
    norm_gain,
    expert_ids,
    affinity,
    gate_weight,
    up_weight,
    down_weight,
):
    seq_count = new_latent.shape[0]
    kv_width = value_up.shape[1]
    head_rows, model_width = out_proj.shape
    half = model_width // 2
    core = lax.axis_index("core")
    planes = SIDE * SIDE
    devices = 2 * SIDE**3
    quarter = model_width // 4

    piece, routes = prepare(out_proj, value_up, expert_ids, affinity)
    one, three = along_y(piece, 1), along_y(piece, -1)
    middle = head_rows // 2
    two_top, two_bottom = along_y(one[:middle], 1), along_y(three[middle:], -1)
    pieces = (piece, one, two_top, two_bottom, three)
    routes, pieces = lax.optimization_barrier((routes, pieces))

    latent = attend(block_table, lengths, queries, new_latent, latent_cache, kv_width)
    outbound = latent.reshape(planes, SIDE * seq_count, kv_width)
    arrived = lax.all_to_all(outbound, PLANE, split_axis=0, concat_axis=0, tiled=True)
    arrived = arrived.reshape(planes * SIDE * seq_count, kv_width)
    placement, mixing = route(routes, devices)
    own_values = find_values(arrived, pieces)
    far_values, placement, mixing = lax.optimization_barrier(
        (other_core(own_values), placement, mixing)
    )
    partial = project(own_values, far_values, pieces, half)

    partial, gate_weight = lax.optimization_barrier((partial, gate_weight))
    far_gate = other_core(gate_weight)
    partial = partial.reshape(2 * planes, seq_count, half)
    collected = lax.all_to_all(partial, ("core",) + PLANE, split_axis=0, concat_axis=0, tiled=True)
    halves = jnp.sum(collected.astype(F32).reshape(2, planes, seq_count, half), axis=1)
    attn_out = jnp.concatenate([halves[0], halves[1]], axis=1)
    attn_out, up_weight, down_weight = lax.optimization_barrier(
        (attn_out, up_weight, down_weight)
    )
    weights = (gate_weight, up_weight, down_weight)
    far_weights = (far_gate, other_core(up_weight), other_core(down_weight))
    mean_square = jnp.mean(attn_out * attn_out, axis=1, keepdims=True)
    normed = (attn_out * lax.rsqrt(mean_square + EPSILON) * norm_gain).astype(BF16)
    parts = jnp.concatenate(
        [normed[:, at : at + quarter] for at in range(0, model_width, quarter)], axis=0
    )
    outgoing = lax.dot_general(
        placement, parts, (((0,), (0,)), ((), ())), preferred_element_type=F32
    )
    outgoing = outgoing.astype(BF16).reshape(devices, 8, quarter)
    received = lax.all_to_all(outgoing, ALL, split_axis=0, concat_axis=0, tiled=True)
    reply = run_expert(received.reshape(devices * 8, quarter), weights, far_weights)
    returned = lax.all_to_all(
        reply.reshape(devices, 8, quarter), ALL, split_axis=0, concat_axis=0, tiled=True
    )
    mixed = dot(mixing, returned.reshape(devices * 8, quarter))
    mixed = mixed[: 4 * seq_count] + mixed[4 * seq_count :]
    mixed = jnp.transpose(mixed.reshape(4, seq_count, quarter), (1, 0, 2))
    expert_out = mixed.reshape(seq_count, model_width).astype(BF16)
    return (normed, expert_out)


def solution(mesh):
    grid = Mesh(mesh.devices.reshape(2, SIDE, SIDE, SIDE), ("core",) + CHIPS)
    rows = P(("core",) + CHIPS, None)
    placed = (
        rows,
        rows,
        rows,
        rows,
        rows,
        P(CHIPS, None, None),
        P(CHIPS, None),
        P(),
        rows,
        rows,
        P(CHIPS, None, "core"),
        P(CHIPS, None, "core"),
        P(CHIPS, "core", None),
    )
    return jax.shard_map(
        shards, mesh=grid, in_specs=placed, out_specs=(rows, rows), check_vma=False
    )
```

```python
import jax
import jax.numpy as jnp
from jax import lax
from jax.experimental import pallas as pl
from jax.experimental.pallas import tpu as pltpu
from jax.sharding import Mesh, PartitionSpec as P

SCORE_SCALE = 192.0 ** (-0.5)
ROUTED_SCALE = 2.5
EPSILON = 1e-06
SIDE = 4
CHIPS = ("z", "x", "y")
PLANE = ("x", "z")
ALL = ("core",) + CHIPS
SWAP = [(0, 1), (1, 0)]
F32 = jnp.float32
BF16 = jnp.bfloat16
MIB = 1 << 20
SMEM = pl.BlockSpec(memory_space=pltpu.SMEM)
VMEM = pl.BlockSpec(memory_space=pltpu.VMEM)
HBM = pl.BlockSpec(memory_space=pltpu.HBM)


def dot_nt(a, b):
    return lax.dot_general(a, b, (((1,), (1,)), ((), ())), preferred_element_type=F32)


def dot(a, b):
    return jnp.dot(a, b, preferred_element_type=F32)


def attend_kernel(
    table_hbm, length_hbm, query_hbm, fresh_hbm, cache_hbm, out_ref,
    table_ref, length_ref, query_ref, fresh_ref, cache_ref, key_ref, sems,
):
    moves = (
        (cache_hbm, cache_ref),
        (query_hbm, query_ref),
        (table_hbm, table_ref),
        (length_hbm, length_ref),
        (fresh_hbm, fresh_ref),
    )
    copies = [pltpu.make_async_copy(a, b, sems.at[i]) for i, (a, b) in enumerate(moves)]
    for copy in copies:
        copy.start()
    seq_count, entry = fresh_ref.shape
    pages = cache_ref.shape[0]
    pairs = cache_ref.shape[1] // (2 * entry)
    wide = entry + 64
    kv_width = out_ref.shape[1]
    spots = pairs * pages
    copies[0].wait()
    for r in range(pairs):
        at = 2 * entry * r
        key_ref[0, r * pages : (r + 1) * pages, :] = cache_ref[:, at : at + wide]
        key_ref[1, r * pages : (r + 1) * pages, :] = cache_ref[:, at + entry - 64 : at + 2 * entry]
    even_keys, odd_keys = key_ref[0], key_ref[1]

    for copy in copies[1:]:
        copy.wait()
    sequence = lax.broadcasted_iota(jnp.int32, (seq_count, spots), 0)
    lane = lax.broadcasted_iota(jnp.int32, (seq_count, spots), 1)
    page, entry_at = lane % pages, 2 * (lane // pages)
    first = jnp.zeros((seq_count, spots), jnp.int32)
    second, live = first, first
    for s in range(seq_count):
        here = sequence == s
        first = jnp.where(here, table_ref[0, 2 * s], first)
        second = jnp.where(here, table_ref[0, 2 * s + 1], second)
        live = jnp.where(here, length_ref[0, s], live)

    def bias_of(position):
        inside = ((page == first) & (position < live)) | (
            (page == second) & (position + 2 * pairs < live)
        )
        return jnp.where(inside, 0.0, -jnp.inf).astype(F32)

    even_bias, odd_bias = bias_of(entry_at), bias_of(entry_at + 1)
    fresh = jnp.concatenate(
        [fresh_ref[...].astype(F32), jnp.zeros((seq_count, wide - entry), F32)], axis=1
    )
    group = 16
    for g in range(query_ref.shape[1] // (2 * entry) // group):
        base = 2 * entry * group * g
        evens = [
            query_ref[:, base + 2 * entry * i : base + 2 * entry * i + wide].astype(F32)
            for i in range(group)
        ]
        odds = [
            query_ref[:, base + 2 * entry * (i + 1) - wide : base + 2 * entry * (i + 1)].astype(F32)
            for i in range(group)
        ]
        rows = group * seq_count
        column = lax.broadcasted_iota(jnp.int32, (rows, wide), 1)
        even_low = jnp.where(column < entry, jnp.concatenate(evens, axis=0), 0.0)
        odd_high = jnp.where(column >= 64, jnp.concatenate(odds, axis=0), 0.0)
        even_high = pltpu.roll(even_low, 64, 1)
        odd_low = pltpu.roll(odd_high, entry, 1)
        low = jnp.concatenate([even_low, odd_low], axis=0)
        high = jnp.concatenate([even_high, odd_high], axis=0)
        heads = 2 * group
        own = jnp.sum(
            low.reshape(heads, seq_count, wide) * fresh[None], axis=2, keepdims=True
        ) * SCORE_SCALE
        even_scores = (dot_nt(low.astype(BF16), even_keys) * SCORE_SCALE).reshape(
            heads, seq_count, spots
        ) + even_bias[None]
        odd_scores = (dot_nt(high.astype(BF16), odd_keys) * SCORE_SCALE).reshape(
            heads, seq_count, spots
        ) + odd_bias[None]
        top = jnp.maximum(
            jnp.max(jnp.maximum(even_scores, odd_scores), axis=2, keepdims=True), own
        )
        even_raised = jnp.exp(even_scores - top)
        odd_raised = jnp.exp(odd_scores - top)
        own_raised = jnp.exp(own - top)
        scale = 1.0 / (
            jnp.sum(even_raised + odd_raised, axis=2, keepdims=True) + own_raised
        )
        even_weights = (even_raised * scale).astype(BF16).reshape(2 * rows, spots)
        odd_weights = (odd_raised * scale).astype(BF16).reshape(2 * rows, spots)
        own_weight = (own_raised * scale).astype(BF16).astype(F32)
        even_part = dot(even_weights, even_keys)[:, :kv_width]
        odd_part = pltpu.roll(dot(odd_weights, odd_keys), entry, 1)[:, :kv_width]
        own_part = (own_weight * fresh[None, :, :kv_width]).reshape(2 * rows, kv_width)
        latent = even_part + odd_part + own_part
        for i in range(group):
            two = jnp.concatenate(
                [
                    latent[i * seq_count : (i + 1) * seq_count],
                    latent[rows + i * seq_count : rows + (i + 1) * seq_count],
                ],
                axis=0,
            )
            head = 2 * (group * g + i)
            across, along, within = head // SIDE**2, head // SIDE % SIDE, head % SIDE
            at = seq_count * ((along * SIDE + across) * SIDE + within)
            out_ref[at : at + 2 * seq_count, :] = two.astype(BF16)


def attend(block_table, lengths, queries, new_latent, latent_cache, kv_width):
    seq_count, entry = new_latent.shape
    head_count = queries.shape[1] // entry
    pages, page_width = latent_cache.shape
    spots = pages * page_width // (2 * entry)
    return pl.pallas_call(
        attend_kernel,
        out_shape=jax.ShapeDtypeStruct((head_count * seq_count, kv_width), BF16),
        in_specs=[HBM] * 5,
        out_specs=VMEM,
        scratch_shapes=[
            pltpu.SMEM(block_table.shape, jnp.int32),
            pltpu.SMEM(lengths.shape, jnp.int32),
            pltpu.VMEM(queries.shape, BF16),
            pltpu.VMEM(new_latent.shape, BF16),
            pltpu.VMEM(latent_cache.shape, BF16),
            pltpu.VMEM((2, spots, entry + 64), BF16),
            pltpu.SemaphoreType.DMA((5,)),
        ],
        compiler_params=pltpu.CompilerParams(vmem_limit_bytes=60 * MIB),
        cost_estimate=pl.CostEstimate(
            flops=1_400_000_000, bytes_accessed=2_400_000, transcendentals=600_000
        ),
        name="attend",
    )(block_table, lengths, queries, new_latent, latent_cache)


def prepare_kernel(out_proj, value_up, ids_hbm, affinity_hbm, piece, routes, ids, affinity, sems):
    core = lax.axis_index("core")
    head_rows, half = out_proj.shape[0], out_proj.shape[1] // 2
    at = pl.ds(pl.multiple_of(core * half, 128), half)
    moves = [
        (ids_hbm, ids),
        (affinity_hbm, affinity),
        (out_proj.at[:, at], piece.at[:, :half]),
    ]
    for b in range(value_up.shape[1] // head_rows):
        rows = pl.ds(b * head_rows, head_rows)
        columns = pl.ds(half + b * head_rows, head_rows)
        moves.append((value_up.at[0, rows], piece.at[:, columns]))
    copies = [pltpu.make_async_copy(a, b, sems.at[i]) for i, (a, b) in enumerate(moves)]
    for copy in copies:
        copy.start()
    for copy in copies[:2]:
        copy.wait()
    rows, top_count = ids.shape
    rest = jnp.zeros((rows, routes.shape[1] - 2 * top_count), F32)
    routes[...] = jnp.concatenate([ids[...].astype(F32), affinity[...], rest], axis=1)
    for copy in copies[2:]:
        copy.wait()


def prepare(out_proj, value_up, expert_ids, affinity):
    head_rows, width = out_proj.shape
    return pl.pallas_call(
        prepare_kernel,
        out_shape=(
            jax.ShapeDtypeStruct((head_rows, width // 2 + value_up.shape[1]), BF16),
            jax.ShapeDtypeStruct((expert_ids.shape[0], 128), F32),
        ),
        in_specs=[HBM] * 4,
        out_specs=(VMEM, VMEM),
        scratch_shapes=[
            pltpu.VMEM(expert_ids.shape, jnp.int32),
            pltpu.VMEM(affinity.shape, F32),
            pltpu.SemaphoreType.DMA((3 + value_up.shape[1] // head_rows,)),
        ],
        compiler_params=pltpu.CompilerParams(vmem_limit_bytes=60 * MIB),
        cost_estimate=pl.CostEstimate(flops=0, bytes_accessed=1_200_000, transcendentals=0),
        name="prepare",
    )(out_proj, value_up, expert_ids, affinity)


def route_kernel(own_ref, place_ref, mix_ref):
    own, top_count = own_ref.shape[0], 8
    tokens = 2 * own
    columns = place_ref.shape[1]
    routes = jnp.concatenate([own_ref[...], own_ref[...]], axis=0)
    affinity = routes[:, top_count : 2 * top_count]
    share = affinity / jnp.sum(affinity, axis=1, keepdims=True) * ROUTED_SCALE
    experts = routes.shape[1]
    expert = lax.broadcasted_iota(jnp.int32, (tokens, experts), 1).astype(F32)
    chosen = jnp.zeros((tokens, experts), F32)
    shares = jnp.zeros((tokens, experts), F32)
    for k in range(top_count):
        hit = expert == routes[:, k : k + 1]
        chosen = jnp.where(hit, 1.0, chosen)
        shares = jnp.where(hit, share[:, k : k + 1], shares)
    row = lax.broadcasted_iota(jnp.int32, (tokens, tokens), 0)
    column = lax.broadcasted_iota(jnp.int32, (tokens, tokens), 1)
    earlier = ((column < row) & (column // own == row // own)).astype(F32)
    rank = dot(earlier.astype(BF16), chosen.astype(BF16))
    slot = (rank + 1.0) * chosen
    named = lax.broadcasted_iota(jnp.int32, (experts, columns), 0)
    at = lax.broadcasted_iota(jnp.int32, (experts, columns), 1)
    each = columns // 2
    spread = (named == at % each // 8 * 2 + at // each).astype(F32).astype(BF16)
    high = shares.astype(BF16)
    low = (shares - high.astype(F32)).astype(BF16)
    at = lax.broadcasted_iota(jnp.int32, (tokens, columns), 1)
    filled = dot(slot.astype(BF16), spread) == (at % 2 + 1).astype(F32)
    high = jnp.where(filled, dot(high, spread), 0.0)
    low = jnp.where(filled, dot(low, spread), 0.0)
    placed = filled.astype(F32)
    quarter = at % 8 // 2

    def by_quarter(table):
        return [jnp.where(quarter == q, table, 0.0)[:own] for q in range(4)]

    place_ref[...] = jnp.concatenate(by_quarter(placed), axis=0).astype(BF16)
    mix_ref[...] = jnp.concatenate(by_quarter(high) + by_quarter(low), axis=0).astype(BF16)


def route(own, devices):
    rows = 4 * own.shape[0]
    return pl.pallas_call(
        route_kernel,
        out_shape=(
            jax.ShapeDtypeStruct((rows, devices * 8), BF16),
            jax.ShapeDtypeStruct((2 * rows, devices * 8), BF16),
        ),
        in_specs=[VMEM],
        out_specs=(VMEM, VMEM),
        compiler_params=pltpu.CompilerParams(vmem_limit_bytes=8 * MIB),
        cost_estimate=pl.CostEstimate(
            flops=20_000_000, bytes_accessed=220_000, transcendentals=0
        ),
        name="route",
    )(own)


def value_kernel(arrived_ref, *refs):
    *piece_refs, out_ref = refs
    place_y = lax.axis_index("y")
    rows, kv_width = arrived_ref.shape
    tokens = rows // SIDE
    head_rows = piece_refs[0].shape[0]
    half = piece_refs[0].shape[1] - kv_width
    to = lax.broadcasted_iota(jnp.int32, (tokens, rows), 0)
    source = lax.broadcasted_iota(jnp.int32, (tokens, rows), 1)
    plane, seq = to // 8, to % 8
    arrived = arrived_ref[...]
    own, one, top, bottom, three = piece_refs
    for k in range(SIDE):
        head = lax.rem(place_y - k + SIDE, SIDE)
        pick = (source == plane * (SIDE * 8) + head * 8 + seq).astype(F32)
        latent = dot(pick.astype(BF16), arrived).astype(BF16)
        total = jnp.zeros((tokens, head_rows), F32)
        for at in range(0, kv_width, head_rows):
            columns = slice(half + at, half + at + head_rows)
            if k == 2:
                up = jnp.concatenate([top[:, columns], bottom[:, columns]], axis=0)
            else:
                up = (own, one, None, three)[k][:, columns]
            total = total + dot(latent[:, at : at + head_rows], up)
        out_ref[:, k * head_rows : (k + 1) * head_rows] = total.astype(BF16)


def find_values(arrived, pieces):
    rows = arrived.shape[0]
    return pl.pallas_call(
        value_kernel,
        out_shape=jax.ShapeDtypeStruct((rows // SIDE, SIDE * pieces[0].shape[0]), BF16),
        in_specs=[VMEM] * 6,
        out_specs=VMEM,
        compiler_params=pltpu.CompilerParams(vmem_limit_bytes=12 * MIB),
        cost_estimate=pl.CostEstimate(
            flops=350_000_000, bytes_accessed=3_200_000, transcendentals=0
        ),
        name="find_values",
    )(arrived, *pieces)


def project_kernel(own_values, far_values, own, one, top, bottom, three, out_ref):
    core = lax.axis_index("core")
    rows, half = own_values.shape[0], out_ref.shape[1]
    mine, theirs = own_values[...].astype(F32), far_values[...].astype(F32)
    values = jnp.concatenate(
        [jnp.where(core == 0, mine, theirs), jnp.where(core == 0, theirs, mine)], axis=0
    ).astype(BF16)
    step = 256
    for at in range(0, half, step):
        columns = slice(at, at + step)
        part = jnp.concatenate([ref[:, columns] for ref in (own, one, top, bottom, three)], axis=0)
        out_ref[:, columns] = dot(values, part).astype(BF16)


def project(own_values, far_values, pieces, half):
    return pl.pallas_call(
        project_kernel,
        out_shape=jax.ShapeDtypeStruct((2 * own_values.shape[0], half), BF16),
        in_specs=[VMEM] * 7,
        out_specs=VMEM,
        compiler_params=pltpu.CompilerParams(vmem_limit_bytes=12 * MIB),
        cost_estimate=pl.CostEstimate(
            flops=600_000_000, bytes_accessed=3_000_000, transcendentals=0
        ),
        name="project",
    )(own_values, far_values, *pieces)


def expert_kernel(
    rows_ref, gate_far, up_far, down_far, gate_near, up_near, down_near, out_ref,
    gate_buf, up_buf, down_buf, wide_ref, total_ref, sems,
):
    core = lax.axis_index("core")
    blocks, width, block = gate_buf.shape
    quarter = width // 4
    count = total_ref.shape[0]

    def copies(i):
        near = i >= blocks // 2
        gate, up, down = (gate_near, up_near, down_near) if near else (gate_far, up_far, down_far)
        at = pl.ds((i % (blocks // 2)) * block, block)
        return (
            pltpu.make_async_copy(gate.at[core, :, at], gate_buf.at[i], sems.at[0, i]),
            pltpu.make_async_copy(up.at[core, :, at], up_buf.at[i], sems.at[1, i]),
            pltpu.make_async_copy(down.at[core, at, :], down_buf.at[i], sems.at[2, i]),
        )

    step = 256
    started = [copies(i) for i in range(blocks)]
    for copy in started[0]:
        copy.start()

    sent = lax.broadcasted_iota(jnp.int32, (256, 256), 1)
    whole = lax.broadcasted_iota(jnp.int32, (256, 256), 0)
    gather = sent == whole % 64 // 2 * 8 + whole // 64 * 2 + whole % 2
    gather = gather.astype(F32).astype(BF16)
    for g in range(count // 64):
        held = dot(gather, rows_ref[g * 256 : (g + 1) * 256, :]).astype(BF16)
        for q in range(4):
            wide_ref[g * 64 : (g + 1) * 64, q * quarter : (q + 1) * quarter] = held[
                q * 64 : (q + 1) * 64
            ]

    for copy in started[1]:
        copy.start()

    for i in range(blocks):
        started[i][0].wait()
        started[i][1].wait()
        if i + 2 < blocks:
            for copy in started[i + 2]:
                copy.start()
        gate = dot(wide_ref[...], gate_buf[i])
        up = dot(wide_ref[...], up_buf[i])
        hidden = (gate / (1.0 + jnp.exp(-gate)) * up).astype(BF16)
        started[i][2].wait()
        for at in range(0, width, 2 * step):
            part = dot(hidden, down_buf[i, :, at : at + 2 * step])
            if i == 0:
                total_ref[:, at : at + 2 * step] = part
            else:
                total_ref[:, at : at + 2 * step] += part

    sent = lax.broadcasted_iota(jnp.int32, (256, 256), 0)
    whole = lax.broadcasted_iota(jnp.int32, (256, 256), 1)
    scatter = sent == whole % 64 // 2 * 8 + whole // 64 * 2 + whole % 2
    scatter = scatter.astype(F32).astype(BF16)
    for g in range(count // 64):
        held = [
            total_ref[g * 64 : (g + 1) * 64, q * quarter : (q + 1) * quarter].astype(BF16)
            for q in range(4)
        ]
        out_ref[g * 256 : (g + 1) * 256, :] = dot(
            scatter, jnp.concatenate(held, axis=0)
        ).astype(BF16)


def run_expert(rows, near, far):
    _, hidden, width = near[2].shape
    count, block = rows.shape[0] // 4, 256
    blocks = 2 * hidden // block
    return pl.pallas_call(
        expert_kernel,
        out_shape=jax.ShapeDtypeStruct(rows.shape, BF16),
        in_specs=[VMEM] + [HBM] * 6,
        out_specs=VMEM,
        scratch_shapes=[
            pltpu.VMEM((blocks, width, block), BF16),
            pltpu.VMEM((blocks, width, block), BF16),
            pltpu.VMEM((blocks, block, width), BF16),
            pltpu.VMEM((count, width), BF16),
            pltpu.VMEM((count, width), F32),
            pltpu.SemaphoreType.DMA((3, blocks)),
        ],
        compiler_params=pltpu.CompilerParams(vmem_limit_bytes=29 * MIB),
        cost_estimate=pl.CostEstimate(
            flops=7_500_000_000, bytes_accessed=26_000_000, transcendentals=300_000
        ),
        name="expert",
    )(rows, *far, *near)


def along_y(array, step):
    return lax.ppermute(array, "y", [(i, (i + step) % SIDE) for i in range(SIDE)])


def other_core(array):
    return lax.ppermute(array, "core", SWAP)


def shards(
    queries,
    new_latent,
    latent_cache,
    block_table,
    lengths,
    value_up,
    out_proj,
    norm_gain,
    expert_ids,
    affinity,
    gate_weight,
    up_weight,
    down_weight,
):
    seq_count = new_latent.shape[0]
    kv_width = value_up.shape[1]
    head_rows, model_width = out_proj.shape
    half = model_width // 2
    core = lax.axis_index("core")
    planes = SIDE * SIDE
    devices = 2 * SIDE**3
    quarter = model_width // 4

    piece, routes = prepare(out_proj, value_up, expert_ids, affinity)
    one, three = along_y(piece, 1), along_y(piece, -1)
    middle = head_rows // 2
    two_top, two_bottom = along_y(one[:middle], 1), along_y(three[middle:], -1)
    pieces = (piece, one, two_top, two_bottom, three)
    routes, pieces = lax.optimization_barrier((routes, pieces))

    latent = attend(block_table, lengths, queries, new_latent, latent_cache, kv_width)
    outbound = latent.reshape(planes, SIDE * seq_count, kv_width)
    arrived = lax.all_to_all(outbound, PLANE, split_axis=0, concat_axis=0, tiled=True)
    arrived = arrived.reshape(planes * SIDE * seq_count, kv_width)
    placement, mixing = route(routes, devices)
    own_values = find_values(arrived, pieces)
    far_values, placement, mixing = lax.optimization_barrier(
        (other_core(own_values), placement, mixing)
    )
    partial = project(own_values, far_values, pieces, half)

    partial = partial.reshape(2 * planes, seq_count, half)
    collected = lax.all_to_all(partial, ("core",) + PLANE, split_axis=0, concat_axis=0, tiled=True)
    halves = jnp.sum(collected.astype(F32).reshape(2, planes, seq_count, half), axis=1)
    attn_out = jnp.concatenate([halves[0], halves[1]], axis=1)
    weights = (gate_weight, up_weight, down_weight)
    attn_out, weights = lax.optimization_barrier((attn_out, weights))
    far_weights = [other_core(w) for w in weights]
    mean_square = jnp.mean(attn_out * attn_out, axis=1, keepdims=True)
    normed = (attn_out * lax.rsqrt(mean_square + EPSILON) * norm_gain).astype(BF16)
    parts = jnp.concatenate(
        [normed[:, at : at + quarter] for at in range(0, model_width, quarter)], axis=0
    )
    outgoing = lax.dot_general(
        placement, parts, (((0,), (0,)), ((), ())), preferred_element_type=F32
    )
    outgoing = outgoing.astype(BF16).reshape(devices, 8, quarter)
    received = lax.all_to_all(outgoing, ALL, split_axis=0, concat_axis=0, tiled=True)
    reply = run_expert(received.reshape(devices * 8, quarter), weights, far_weights)
    returned = lax.all_to_all(
        reply.reshape(devices, 8, quarter), ALL, split_axis=0, concat_axis=0, tiled=True
    )
    mixed = dot(mixing, returned.reshape(devices * 8, quarter))
    mixed = mixed[: 4 * seq_count] + mixed[4 * seq_count :]
    mixed = jnp.transpose(mixed.reshape(4, seq_count, quarter), (1, 0, 2))
    expert_out = mixed.reshape(seq_count, model_width).astype(BF16)
    return (normed, expert_out)


def solution(mesh):
    grid = Mesh(mesh.devices.reshape(2, SIDE, SIDE, SIDE), ("core",) + CHIPS)
    rows = P(("core",) + CHIPS, None)
    placed = (
        rows,
        rows,
        rows,
        rows,
        rows,
        P(CHIPS, None, None),
        P(CHIPS, None),
        P(),
        rows,
        rows,
        P(CHIPS, None, "core"),
        P(CHIPS, None, "core"),
        P(CHIPS, "core", None),
    )
    return jax.shard_map(
        shards, mesh=grid, in_specs=placed, out_specs=(rows, rows), check_vma=False
    )
```

```python
import jax
import jax.numpy as jnp
from jax import lax
from jax.experimental import pallas as pl
from jax.experimental.pallas import tpu as pltpu
from jax.sharding import Mesh, PartitionSpec as P

SCORE_SCALE = 192.0 ** (-0.5)
ROUTED_SCALE = 2.5
EPSILON = 1e-06
SIDE = 4
CHIPS = ("z", "x", "y")
PLANE = ("x", "z")
ALL = ("core",) + CHIPS
SWAP = [(0, 1), (1, 0)]
F32 = jnp.float32
BF16 = jnp.bfloat16
MIB = 1 << 20
SMEM = pl.BlockSpec(memory_space=pltpu.SMEM)
VMEM = pl.BlockSpec(memory_space=pltpu.VMEM)
HBM = pl.BlockSpec(memory_space=pltpu.HBM)


def dot_nt(a, b):
    return lax.dot_general(a, b, (((1,), (1,)), ((), ())), preferred_element_type=F32)


def dot(a, b):
    return jnp.dot(a, b, preferred_element_type=F32)


def attend_kernel(
    table_hbm, length_hbm, query_hbm, fresh_hbm, cache_hbm, out_ref,
    table_ref, length_ref, query_ref, fresh_ref, cache_ref, key_ref, sems,
):
    moves = (
        (cache_hbm, cache_ref),
        (query_hbm, query_ref),
        (table_hbm, table_ref),
        (length_hbm, length_ref),
        (fresh_hbm, fresh_ref),
    )
    copies = [pltpu.make_async_copy(a, b, sems.at[i]) for i, (a, b) in enumerate(moves)]
    for copy in copies:
        copy.start()
    seq_count, entry = fresh_ref.shape
    pages = cache_ref.shape[0]
    pairs = cache_ref.shape[1] // (2 * entry)
    wide = entry + 64
    kv_width = out_ref.shape[1]
    spots = pairs * pages
    copies[0].wait()
    for r in range(pairs):
        at = 2 * entry * r
        key_ref[0, r * pages : (r + 1) * pages, :] = cache_ref[:, at : at + wide]
        key_ref[1, r * pages : (r + 1) * pages, :] = cache_ref[:, at + entry - 64 : at + 2 * entry]
    even_keys, odd_keys = key_ref[0], key_ref[1]

    for copy in copies[1:]:
        copy.wait()
    sequence = lax.broadcasted_iota(jnp.int32, (seq_count, spots), 0)
    lane = lax.broadcasted_iota(jnp.int32, (seq_count, spots), 1)
    page, entry_at = lane % pages, 2 * (lane // pages)
    first = jnp.zeros((seq_count, spots), jnp.int32)
    second, live = first, first
    for s in range(seq_count):
        here = sequence == s
        first = jnp.where(here, table_ref[0, 2 * s], first)
        second = jnp.where(here, table_ref[0, 2 * s + 1], second)
        live = jnp.where(here, length_ref[0, s], live)

    def bias_of(position):
        inside = ((page == first) & (position < live)) | (
            (page == second) & (position + 2 * pairs < live)
        )
        return jnp.where(inside, 0.0, -jnp.inf).astype(F32)

    even_bias, odd_bias = bias_of(entry_at), bias_of(entry_at + 1)
    fresh = jnp.concatenate(
        [fresh_ref[...].astype(F32), jnp.zeros((seq_count, wide - entry), F32)], axis=1
    )
    group = 16
    for g in range(query_ref.shape[1] // (2 * entry) // group):
        base = 2 * entry * group * g
        evens = [
            query_ref[:, base + 2 * entry * i : base + 2 * entry * i + wide].astype(F32)
            for i in range(group)
        ]
        odds = [
            query_ref[:, base + 2 * entry * (i + 1) - wide : base + 2 * entry * (i + 1)].astype(F32)
            for i in range(group)
        ]
        rows = group * seq_count
        column = lax.broadcasted_iota(jnp.int32, (rows, wide), 1)
        even_low = jnp.where(column < entry, jnp.concatenate(evens, axis=0), 0.0)
        odd_high = jnp.where(column >= 64, jnp.concatenate(odds, axis=0), 0.0)
        even_high = pltpu.roll(even_low, 64, 1)
        odd_low = pltpu.roll(odd_high, entry, 1)
        low = jnp.concatenate([even_low, odd_low], axis=0)
        high = jnp.concatenate([even_high, odd_high], axis=0)
        heads = 2 * group
        own = jnp.sum(
            low.reshape(heads, seq_count, wide) * fresh[None], axis=2, keepdims=True
        ) * SCORE_SCALE
        even_scores = (dot_nt(low.astype(BF16), even_keys) * SCORE_SCALE).reshape(
            heads, seq_count, spots
        ) + even_bias[None]
        odd_scores = (dot_nt(high.astype(BF16), odd_keys) * SCORE_SCALE).reshape(
            heads, seq_count, spots
        ) + odd_bias[None]
        top = jnp.maximum(
            jnp.max(jnp.maximum(even_scores, odd_scores), axis=2, keepdims=True), own
        )
        even_raised = jnp.exp(even_scores - top)
        odd_raised = jnp.exp(odd_scores - top)
        own_raised = jnp.exp(own - top)
        scale = 1.0 / (
            jnp.sum(even_raised + odd_raised, axis=2, keepdims=True) + own_raised
        )
        even_weights = (even_raised * scale).astype(BF16).reshape(2 * rows, spots)
        odd_weights = (odd_raised * scale).astype(BF16).reshape(2 * rows, spots)
        own_weight = (own_raised * scale).astype(BF16).astype(F32)
        even_part = dot(even_weights, even_keys)[:, :kv_width]
        odd_part = pltpu.roll(dot(odd_weights, odd_keys), entry, 1)[:, :kv_width]
        own_part = (own_weight * fresh[None, :, :kv_width]).reshape(2 * rows, kv_width)
        latent = even_part + odd_part + own_part
        for i in range(group):
            two = jnp.concatenate(
                [
                    latent[i * seq_count : (i + 1) * seq_count],
                    latent[rows + i * seq_count : rows + (i + 1) * seq_count],
                ],
                axis=0,
            )
            head = 2 * (group * g + i)
            across, along, within = head // SIDE**2, head // SIDE % SIDE, head % SIDE
            at = seq_count * ((along * SIDE + across) * SIDE + within)
            out_ref[at : at + 2 * seq_count, :] = two.astype(BF16)


def attend(block_table, lengths, queries, new_latent, latent_cache, kv_width):
    seq_count, entry = new_latent.shape
    head_count = queries.shape[1] // entry
    pages, page_width = latent_cache.shape
    spots = pages * page_width // (2 * entry)
    return pl.pallas_call(
        attend_kernel,
        out_shape=jax.ShapeDtypeStruct((head_count * seq_count, kv_width), BF16),
        in_specs=[HBM] * 5,
        out_specs=VMEM,
        scratch_shapes=[
            pltpu.SMEM(block_table.shape, jnp.int32),
            pltpu.SMEM(lengths.shape, jnp.int32),
            pltpu.VMEM(queries.shape, BF16),
            pltpu.VMEM(new_latent.shape, BF16),
            pltpu.VMEM(latent_cache.shape, BF16),
            pltpu.VMEM((2, spots, entry + 64), BF16),
            pltpu.SemaphoreType.DMA((5,)),
        ],
        compiler_params=pltpu.CompilerParams(vmem_limit_bytes=60 * MIB),
        cost_estimate=pl.CostEstimate(
            flops=1_400_000_000, bytes_accessed=2_400_000, transcendentals=600_000
        ),
        name="attend",
    )(block_table, lengths, queries, new_latent, latent_cache)


def prepare_kernel(out_proj, value_up, ids_hbm, affinity_hbm, piece, routes, ids, affinity, sems):
    core = lax.axis_index("core")
    head_rows, half = out_proj.shape[0], out_proj.shape[1] // 2
    at = pl.ds(pl.multiple_of(core * half, 128), half)
    moves = [
        (ids_hbm, ids),
        (affinity_hbm, affinity),
        (out_proj.at[:, at], piece.at[:, :half]),
    ]
    for b in range(value_up.shape[1] // head_rows):
        rows = pl.ds(b * head_rows, head_rows)
        columns = pl.ds(half + b * head_rows, head_rows)
        moves.append((value_up.at[0, rows], piece.at[:, columns]))
    copies = [pltpu.make_async_copy(a, b, sems.at[i]) for i, (a, b) in enumerate(moves)]
    for copy in copies:
        copy.start()
    for copy in copies[:2]:
        copy.wait()
    rows, top_count = ids.shape
    rest = jnp.zeros((rows, routes.shape[1] - 2 * top_count), F32)
    routes[...] = jnp.concatenate([ids[...].astype(F32), affinity[...], rest], axis=1)
    for copy in copies[2:]:
        copy.wait()


def prepare(out_proj, value_up, expert_ids, affinity):
    head_rows, width = out_proj.shape
    return pl.pallas_call(
        prepare_kernel,
        out_shape=(
            jax.ShapeDtypeStruct((head_rows, width // 2 + value_up.shape[1]), BF16),
            jax.ShapeDtypeStruct((expert_ids.shape[0], 128), F32),
        ),
        in_specs=[HBM] * 4,
        out_specs=(VMEM, VMEM),
        scratch_shapes=[
            pltpu.VMEM(expert_ids.shape, jnp.int32),
            pltpu.VMEM(affinity.shape, F32),
            pltpu.SemaphoreType.DMA((3 + value_up.shape[1] // head_rows,)),
        ],
        compiler_params=pltpu.CompilerParams(vmem_limit_bytes=60 * MIB),
        cost_estimate=pl.CostEstimate(flops=0, bytes_accessed=1_200_000, transcendentals=0),
        name="prepare",
    )(out_proj, value_up, expert_ids, affinity)


def route_kernel(own_ref, place_ref, mix_ref):
    own, top_count = own_ref.shape[0], 8
    tokens = 2 * own
    columns = place_ref.shape[1]
    routes = jnp.concatenate([own_ref[...], own_ref[...]], axis=0)
    affinity = routes[:, top_count : 2 * top_count]
    share = affinity / jnp.sum(affinity, axis=1, keepdims=True) * ROUTED_SCALE
    experts = routes.shape[1]
    expert = lax.broadcasted_iota(jnp.int32, (tokens, experts), 1).astype(F32)
    chosen = jnp.zeros((tokens, experts), F32)
    shares = jnp.zeros((tokens, experts), F32)
    for k in range(top_count):
        hit = expert == routes[:, k : k + 1]
        chosen = jnp.where(hit, 1.0, chosen)
        shares = jnp.where(hit, share[:, k : k + 1], shares)
    row = lax.broadcasted_iota(jnp.int32, (tokens, tokens), 0)
    column = lax.broadcasted_iota(jnp.int32, (tokens, tokens), 1)
    earlier = ((column < row) & (column // own == row // own)).astype(F32)
    rank = dot(earlier.astype(BF16), chosen.astype(BF16))
    slot = (rank + 1.0) * chosen
    named = lax.broadcasted_iota(jnp.int32, (experts, columns), 0)
    at = lax.broadcasted_iota(jnp.int32, (experts, columns), 1)
    each = columns // 2
    spread = (named == at % each // 8 * 2 + at // each).astype(F32).astype(BF16)
    high = shares.astype(BF16)
    low = (shares - high.astype(F32)).astype(BF16)
    at = lax.broadcasted_iota(jnp.int32, (tokens, columns), 1)
    filled = dot(slot.astype(BF16), spread) == (at % 2 + 1).astype(F32)
    high = jnp.where(filled, dot(high, spread), 0.0)
    low = jnp.where(filled, dot(low, spread), 0.0)
    placed = filled.astype(F32)
    quarter = at % 8 // 2

    def by_quarter(table):
        return [jnp.where(quarter == q, table, 0.0)[:own] for q in range(4)]

    place_ref[...] = jnp.concatenate(by_quarter(placed), axis=0).astype(BF16)
    mix_ref[...] = jnp.concatenate(by_quarter(high) + by_quarter(low), axis=0).astype(BF16)


def route(own, devices):
    rows = 4 * own.shape[0]
    return pl.pallas_call(
        route_kernel,
        out_shape=(
            jax.ShapeDtypeStruct((rows, devices * 8), BF16),
            jax.ShapeDtypeStruct((2 * rows, devices * 8), BF16),
        ),
        in_specs=[VMEM],
        out_specs=(VMEM, VMEM),
        compiler_params=pltpu.CompilerParams(vmem_limit_bytes=8 * MIB),
        cost_estimate=pl.CostEstimate(
            flops=20_000_000, bytes_accessed=220_000, transcendentals=0
        ),
        name="route",
    )(own)


def value_kernel(arrived_ref, *refs):
    *piece_refs, out_ref = refs
    place_y = lax.axis_index("y")
    rows, kv_width = arrived_ref.shape
    tokens = rows // SIDE
    head_rows = piece_refs[0].shape[0]
    half = piece_refs[0].shape[1] - kv_width
    to = lax.broadcasted_iota(jnp.int32, (tokens, rows), 0)
    source = lax.broadcasted_iota(jnp.int32, (tokens, rows), 1)
    plane, seq = to // 8, to % 8
    arrived = arrived_ref[...]
    own, one, top, bottom, three = piece_refs
    for k in range(SIDE):
        head = lax.rem(place_y - k + SIDE, SIDE)
        pick = (source == plane * (SIDE * 8) + head * 8 + seq).astype(F32)
        latent = dot(pick.astype(BF16), arrived).astype(BF16)
        blocks = []
        for at in range(half, half + kv_width, head_rows):
            columns = slice(at, at + head_rows)
            if k == 2:
                blocks += [top[:, columns], bottom[:, columns]]
            else:
                blocks.append((own, one, None, three)[k][:, columns])
        total = dot(latent, jnp.concatenate(blocks, axis=0))
        out_ref[:, k * head_rows : (k + 1) * head_rows] = total.astype(BF16)


def find_values(arrived, pieces):
    rows = arrived.shape[0]
    return pl.pallas_call(
        value_kernel,
        out_shape=jax.ShapeDtypeStruct((rows // SIDE, SIDE * pieces[0].shape[0]), BF16),
        in_specs=[VMEM] * 6,
        out_specs=VMEM,
        compiler_params=pltpu.CompilerParams(vmem_limit_bytes=12 * MIB),
        cost_estimate=pl.CostEstimate(
            flops=350_000_000, bytes_accessed=3_200_000, transcendentals=0
        ),
        name="find_values",
    )(arrived, *pieces)


def project_kernel(own_values, far_values, own, one, top, bottom, three, out_ref):
    core = lax.axis_index("core")
    rows, half = own_values.shape[0], out_ref.shape[1]
    mine, theirs = own_values[...].astype(F32), far_values[...].astype(F32)
    values = jnp.concatenate(
        [jnp.where(core == 0, mine, theirs), jnp.where(core == 0, theirs, mine)], axis=0
    ).astype(BF16)
    step = 256
    for at in range(0, half, step):
        columns = slice(at, at + step)
        part = jnp.concatenate([ref[:, columns] for ref in (own, one, top, bottom, three)], axis=0)
        out_ref[:, columns] = dot(values, part).astype(BF16)


def project(own_values, far_values, pieces, half):
    return pl.pallas_call(
        project_kernel,
        out_shape=jax.ShapeDtypeStruct((2 * own_values.shape[0], half), BF16),
        in_specs=[VMEM] * 7,
        out_specs=VMEM,
        compiler_params=pltpu.CompilerParams(vmem_limit_bytes=12 * MIB),
        cost_estimate=pl.CostEstimate(
            flops=600_000_000, bytes_accessed=3_000_000, transcendentals=0
        ),
        name="project",
    )(own_values, far_values, *pieces)


def expert_kernel(
    rows_ref, gate_far, up_far, down_far, gate_near, up_near, down_near, out_ref,
    gate_buf, up_buf, down_buf, wide_ref, total_ref, sems,
):
    core = lax.axis_index("core")
    blocks, width, block = gate_buf.shape
    quarter = width // 4
    count = total_ref.shape[0]

    def copies(i):
        near = i >= blocks // 2
        gate, up, down = (gate_near, up_near, down_near) if near else (gate_far, up_far, down_far)
        at = pl.ds((i % (blocks // 2)) * block, block)
        return (
            pltpu.make_async_copy(gate.at[core, :, at], gate_buf.at[i], sems.at[0, i]),
            pltpu.make_async_copy(up.at[core, :, at], up_buf.at[i], sems.at[1, i]),
            pltpu.make_async_copy(down.at[core, at, :], down_buf.at[i], sems.at[2, i]),
        )

    step = 256
    started = [copies(i) for i in range(blocks)]
    for copy in started[0]:
        copy.start()

    sent = lax.broadcasted_iota(jnp.int32, (256, 256), 1)
    whole = lax.broadcasted_iota(jnp.int32, (256, 256), 0)
    gather = sent == whole % 64 // 2 * 8 + whole // 64 * 2 + whole % 2
    gather = gather.astype(F32).astype(BF16)
    for g in range(count // 64):
        held = dot(gather, rows_ref[g * 256 : (g + 1) * 256, :]).astype(BF16)
        for q in range(4):
            wide_ref[g * 64 : (g + 1) * 64, q * quarter : (q + 1) * quarter] = held[
                q * 64 : (q + 1) * 64
            ]

    for copy in started[1]:
        copy.start()

    for i in range(blocks):
        started[i][0].wait()
        started[i][1].wait()
        if i + 2 < blocks:
            for copy in started[i + 2]:
                copy.start()
        gate = dot(wide_ref[...], gate_buf[i])
        up = dot(wide_ref[...], up_buf[i])
        hidden = (gate / (1.0 + jnp.exp(-gate)) * up).astype(BF16)
        started[i][2].wait()
        for at in range(0, width, 2 * step):
            part = dot(hidden, down_buf[i, :, at : at + 2 * step])
            if i == 0:
                total_ref[:, at : at + 2 * step] = part
            else:
                total_ref[:, at : at + 2 * step] += part

    sent = lax.broadcasted_iota(jnp.int32, (256, 256), 0)
    whole = lax.broadcasted_iota(jnp.int32, (256, 256), 1)
    scatter = sent == whole % 64 // 2 * 8 + whole // 64 * 2 + whole % 2
    scatter = scatter.astype(F32).astype(BF16)
    for g in range(count // 64):
        held = [
            total_ref[g * 64 : (g + 1) * 64, q * quarter : (q + 1) * quarter].astype(BF16)
            for q in range(4)
        ]
        out_ref[g * 256 : (g + 1) * 256, :] = dot(
            scatter, jnp.concatenate(held, axis=0)
        ).astype(BF16)


def run_expert(rows, near, far):
    _, hidden, width = near[2].shape
    count, block = rows.shape[0] // 4, 256
    blocks = 2 * hidden // block
    return pl.pallas_call(
        expert_kernel,
        out_shape=jax.ShapeDtypeStruct(rows.shape, BF16),
        in_specs=[VMEM] + [HBM] * 6,
        out_specs=VMEM,
        scratch_shapes=[
            pltpu.VMEM((blocks, width, block), BF16),
            pltpu.VMEM((blocks, width, block), BF16),
            pltpu.VMEM((blocks, block, width), BF16),
            pltpu.VMEM((count, width), BF16),
            pltpu.VMEM((count, width), F32),
            pltpu.SemaphoreType.DMA((3, blocks)),
        ],
        compiler_params=pltpu.CompilerParams(vmem_limit_bytes=29 * MIB),
        cost_estimate=pl.CostEstimate(
            flops=7_500_000_000, bytes_accessed=26_000_000, transcendentals=300_000
        ),
        name="expert",
    )(rows, *far, *near)


def along_y(array, step):
    return lax.ppermute(array, "y", [(i, (i + step) % SIDE) for i in range(SIDE)])


def other_core(array):
    return lax.ppermute(array, "core", SWAP)


def shards(
    queries,
    new_latent,
    latent_cache,
    block_table,
    lengths,
    value_up,
    out_proj,
    norm_gain,
    expert_ids,
    affinity,
    gate_weight,
    up_weight,
    down_weight,
):
    seq_count = new_latent.shape[0]
    kv_width = value_up.shape[1]
    head_rows, model_width = out_proj.shape
    half = model_width // 2
    core = lax.axis_index("core")
    planes = SIDE * SIDE
    devices = 2 * SIDE**3
    quarter = model_width // 4

    piece, routes = prepare(out_proj, value_up, expert_ids, affinity)
    one, three = along_y(piece, 1), along_y(piece, -1)
    middle = head_rows // 2
    two_top, two_bottom = along_y(one[:middle], 1), along_y(three[middle:], -1)
    pieces = (piece, one, two_top, two_bottom, three)
    routes, pieces = lax.optimization_barrier((routes, pieces))

    latent = attend(block_table, lengths, queries, new_latent, latent_cache, kv_width)
    outbound = latent.reshape(planes, SIDE * seq_count, kv_width)
    arrived = lax.all_to_all(outbound, PLANE, split_axis=0, concat_axis=0, tiled=True)
    arrived = arrived.reshape(planes * SIDE * seq_count, kv_width)
    placement, mixing = route(routes, devices)
    own_values = find_values(arrived, pieces)
    far_values, placement, mixing = lax.optimization_barrier(
        (other_core(own_values), placement, mixing)
    )
    partial = project(own_values, far_values, pieces, half)

    partial = partial.reshape(2 * planes, seq_count, half)
    collected = lax.all_to_all(partial, ("core",) + PLANE, split_axis=0, concat_axis=0, tiled=True)
    halves = jnp.sum(collected.astype(F32).reshape(2, planes, seq_count, half), axis=1)
    attn_out = jnp.concatenate([halves[0], halves[1]], axis=1)
    weights = (gate_weight, up_weight, down_weight)
    attn_out, weights = lax.optimization_barrier((attn_out, weights))
    far_weights = [other_core(w) for w in weights]
    mean_square = jnp.mean(attn_out * attn_out, axis=1, keepdims=True)
    normed = (attn_out * lax.rsqrt(mean_square + EPSILON) * norm_gain).astype(BF16)
    parts = jnp.concatenate(
        [normed[:, at : at + quarter] for at in range(0, model_width, quarter)], axis=0
    )
    outgoing = lax.dot_general(
        placement, parts, (((0,), (0,)), ((), ())), preferred_element_type=F32
    )
    outgoing = outgoing.astype(BF16).reshape(devices, 8, quarter)
    received = lax.all_to_all(outgoing, ALL, split_axis=0, concat_axis=0, tiled=True)
    reply = run_expert(received.reshape(devices * 8, quarter), weights, far_weights)
    returned = lax.all_to_all(
        reply.reshape(devices, 8, quarter), ALL, split_axis=0, concat_axis=0, tiled=True
    )
    mixed = dot(mixing, returned.reshape(devices * 8, quarter))
    mixed = mixed[: 4 * seq_count] + mixed[4 * seq_count :]
    mixed = jnp.transpose(mixed.reshape(4, seq_count, quarter), (1, 0, 2))
    expert_out = mixed.reshape(seq_count, model_width).astype(BF16)
    return (normed, expert_out)


def solution(mesh):
    grid = Mesh(mesh.devices.reshape(2, SIDE, SIDE, SIDE), ("core",) + CHIPS)
    rows = P(("core",) + CHIPS, None)
    placed = (
        rows,
        rows,
        rows,
        rows,
        rows,
        P(CHIPS, None, None),
        P(CHIPS, None),
        P(),
        rows,
        rows,
        P(CHIPS, None, "core"),
        P(CHIPS, None, "core"),
        P(CHIPS, "core", None),
    )
    return jax.shard_map(
        shards, mesh=grid, in_specs=placed, out_specs=(rows, rows), check_vma=False
    )
```
